32 devices in a mesh: rep: 8 (over z, y), ch: 4 (over x, core).
Axes of the slice: x: 2, y: 2, z: 4, core: 2. Of those that a mesh axis runs over, the one named last changes fastest.
Arguments:
- patches: bfloat16 [8, 768, 4352], P('rep', 'ch'), may hold values from -28 to 28
- cotangents: bfloat16 [8, 768, 2688], P('rep', 'ch'), may hold values from -0.06 to 0.06
- weight: float32 [768, 27, 768], P(('ch', 'rep')), may hold values from -0.0390625 to 0.0390625
- momentum: float32 [768, 27, 768], P(('ch', 'rep')), may hold values from -6 to 6
Outputs:
- new_weight: float32 [768, 27, 768], P(('ch', 'rep'))
- new_momentum: float32 [768, 27, 768], P(('ch', 'rep'))
The draws below stay inside these ranges and needn't reach their ends.
All inputs are finite; a program needn't handle non-finite values.
Results may differ from the reference program's by a relative error of at most 0.0003.
Values may be sent and summed in bfloat16 or wider, within the bound.
No kernel may reach another device: no remote copies, remote signals or barrier semaphores. Data moves between devices by JAX's collectives and lax.ppermute only.
A program may use at most 128 MiB of HBM per device.

```python
import math
import jax
import jax.numpy as jnp
from jax import lax

C_IN = 768
C_OUT = 768
KERNEL = 3
DEPTH = 6
HEIGHT = 14
WIDTH = 32
VOX = 2688
TAPS = 27
LEVELS = 3
N_REP = 8
N_CH = 4


def draw_patches(key, part):
    span_cells = (DEPTH + KERNEL - 1) * (HEIGHT + KERNEL - 1) * (WIDTH + KERNEL - 1)
    shape_one = (1, C_IN, span_cells)
    full_shape = (N_REP, C_IN, span_cells)
    common = jnp.clip(jax.random.normal(jax.random.fold_in(key, 11), shape_one, jnp.float32), -4.0, 4.0)
    own_part = jnp.clip(jax.random.normal(jax.random.fold_in(key, 12), full_shape, jnp.float32), -4.0, 4.0)
    shared = 0.8
    scales = jnp.exp(jax.random.uniform(jax.random.fold_in(key, 13), (C_IN,), jnp.float32, math.log(0.5), math.log(5.0)))
    values = scales[None, :, None] * (shared * common + math.sqrt(1.0 - shared * shared) * own_part)
    return values.astype(jnp.bfloat16)


def draw_cotangents(key, part):
    voxels = DEPTH * HEIGHT * WIDTH
    shape_one = (1, C_OUT, voxels)
    full_shape = (N_REP, C_OUT, voxels)
    common = jnp.clip(jax.random.normal(jax.random.fold_in(key, 21), shape_one, jnp.float32), -4.0, 4.0)
    own_part = jnp.clip(jax.random.normal(jax.random.fold_in(key, 22), full_shape, jnp.float32), -4.0, 4.0)
    local_count = C_OUT // N_CH
    channel_ids = jnp.arange(C_OUT)
    position = (channel_ids % local_count).astype(jnp.float32) / max(local_count - 1, 1)
    ramp = channel_ids.astype(jnp.float32) / max(C_OUT - 1, 1)
    jitter = jax.random.uniform(jax.random.fold_in(key, 23), (C_OUT,), jnp.float32, -0.05, 0.05)
    shared = (0.3 + 0.6 * jnp.abs(2.0 * position - 1.0) + jitter)[None, :, None]
    slope_jitter = jax.random.uniform(jax.random.fold_in(key, 25), (C_OUT,), jnp.float32, -0.2, 0.2)
    direction = 2.0 * (2.0 * position - 1.0) + slope_jitter
    replica_pos = jnp.arange(N_REP).astype(jnp.float32) / max(N_REP - 1, 1) - 0.5
    replica_scale = jnp.exp(math.log(3.0) * replica_pos[:, None] * direction[None, :])
    channel_scale = (1.0 + 2.0 * ramp) * jnp.exp(jax.random.uniform(jax.random.fold_in(key, 24), (C_OUT,), jnp.float32, 0.0, math.log(2.0)))
    values = 0.0005 * replica_scale[:, :, None] * channel_scale[None, :, None] * (shared * common + jnp.sqrt(1.0 - shared * shared) * own_part)
    return values.astype(jnp.bfloat16)


def shard_levels(rng, extent, split, least, top_value):
    level, own = 1.0, jax.random.fold_in(rng, 6)
    for dim, shards_of in split:
        heights = jnp.exp(jax.random.uniform(jax.random.fold_in(own, dim), (shards_of,), jnp.float32, least / len(split), top_value / len(split)))
        level = level * jnp.repeat(heights, extent[dim] // shards_of).reshape([-1 if axis == dim else 1 for axis in range(len(extent))])
    return level


def normal_values(stream_key, shape, spread, bound, cuts=(), kind=jnp.bfloat16):
    gain = shard_levels(stream_key, shape, cuts, -0.22, 0.18) if cuts else 1.0
    result = jax.random.normal(stream_key, shape, jnp.float32) * spread * gain
    return jnp.minimum(jnp.maximum(result, -bound), bound).astype(kind)


def setup_inputs(seed: int = 0) -> dict:
    splits = jax.random.split(jax.random.key(seed), 5)
    return {
        "patches": draw_patches(jax.random.fold_in(splits[4], 71), 0),
        "cotangents": draw_cotangents(jax.random.fold_in(splits[4], 71), 0),
        "weight": normal_values(splits[2], (C_OUT, TAPS, C_IN), (TAPS * C_IN) ** -0.5, 0.0390625, ((0, 32),), jnp.float32),
        "momentum": normal_values(splits[3], (C_OUT, TAPS, C_IN), 1.0, 6.0, ((0, 32),), jnp.float32),
    }


momentum_decay = 0.9
learning_rate = 0.05

def replica_gradient(patch, cotangent):
    flat_cot = cotangent.astype(jnp.float32)
    volume = patch.reshape(C_IN, DEPTH + KERNEL - 1, HEIGHT + KERNEL - 1, WIDTH + KERNEL - 1)

    def one_tap(tap_index):
        first_off = tap_index // (KERNEL * KERNEL)
        second_off = tap_index // KERNEL % KERNEL
        third_off = tap_index % KERNEL
        window = lax.dynamic_slice(volume, (jnp.int32(0), first_off, second_off, third_off), (C_IN, DEPTH, HEIGHT, WIDTH))
        window = window.astype(jnp.float32).reshape(C_IN, VOX)
        return jnp.dot(flat_cot, window.T, precision=lax.Precision.HIGHEST, preferred_element_type=jnp.float32)
    per_tap = lax.map(one_tap, jnp.arange(TAPS, dtype=jnp.int32))
    return jnp.transpose(per_tap, (1, 0, 2))

def adasum_pair(former, latter):
    inner = jnp.sum(former * latter)
    former_sq = jnp.sum(former * former)
    latter_sq = jnp.sum(latter * latter)
    return (1.0 - inner / (2.0 * former_sq)) * former + (1.0 - inner / (2.0 * latter_sq)) * latter

def reference(patches, cotangents, weight, momentum):

    def leaf_grad(replica):
        return replica_gradient(patches[replica], cotangents[replica])

    def combine(low_bits, depth_bits):
        if depth_bits == LEVELS:
            return leaf_grad(low_bits)
        return adasum_pair(combine(low_bits, depth_bits + 1), combine(low_bits + 2 ** depth_bits, depth_bits + 1))
    combined = combine(0, 0)
    new_momentum = momentum_decay * momentum + combined
    new_weight = weight - learning_rate * new_momentum
    return (new_weight, new_momentum)
```

```python
import jax
import jax.numpy as jnp
from jax import lax
from jax.experimental import pallas as pl
from jax.experimental.pallas import tpu as pltpu
from jax.sharding import PartitionSpec as P

KERNEL = 3
DEPTH = 6
HEIGHT = 14
WIDTH = 32
ROWS = HEIGHT + KERNEL - 1
CELLS = WIDTH + KERNEL - 1
PLANES = DEPTH + KERNEL - 1
SPAN = ROWS * WIDTH
LANES = 128
PER_VREG = LANES // WIDTH

momentum_decay = 0.9
learning_rate = 0.05

BF16 = jnp.bfloat16
F32 = jnp.float32
VMEM = pl.BlockSpec(memory_space=pltpu.VMEM)
SMEM = pl.BlockSpec(memory_space=pltpu.SMEM)
PARAMS = pltpu.CompilerParams(vmem_limit_bytes=56 * 2**20)


def swap(value, axis, mask):
    pairs = [(source, source ^ mask) for source in range(lax.axis_size(axis))]
    return lax.ppermute(value, axis, pairs)


def swap_both(value, rep_mask, ch_mask):
    reps, chs = lax.axis_size("rep"), lax.axis_size("ch")
    pairs = [
        (r * chs + c, (r ^ rep_mask) * chs + (c ^ ch_mask))
        for r in range(reps)
        for c in range(chs)
    ]
    return lax.ppermute(value, ("rep", "ch"), pairs)


def pack_kernel(low, patch_ref, *refs):
    parts, buf = refs[:-1], refs[-1]
    main = PLANES * SPAN
    for row in range(PLANES * ROWS):
        buf[:, WIDTH * row : WIDTH * (row + 1)] = patch_ref[:, CELLS * row : CELLS * row + WIDTH]
    total = PLANES * ROWS * CELLS
    tail = 2 * LANES
    k = lax.broadcasted_iota(jnp.int32, (total, tail), 0)
    n = lax.broadcasted_iota(jnp.int32, (total, tail), 1)
    lane = n % LANES
    row = PER_VREG * (lane % WIDTH) + lane // WIDTH
    pick = (k == row * CELLS + WIDTH + n // LANES).astype(BF16)
    buf[:, main:] = jnp.dot(patch_ref[...], pick, preferred_element_type=F32).astype(BF16)
    size = parts[0].shape[0]
    for mask, out in enumerate(parts):
        start = pl.multiple_of(jnp.bitwise_xor(low[0], mask) * size, 16)
        out[...] = buf[pl.ds(start, size), :]


def pack_patch(low, patch, parts):
    size = -(-patch.shape[0] // (16 * parts)) * 16
    if size * parts != patch.shape[0]:
        by_part = patch.reshape(parts, -1, patch.shape[1])
        by_part = jnp.pad(by_part, ((0, 0), (0, size - by_part.shape[1]), (0, 0)))
        patch = by_part.reshape(parts * size, -1)
    channels, total = patch.shape
    shape = jax.ShapeDtypeStruct((channels // parts, total), BF16)
    return pl.pallas_call(
        pack_kernel,
        out_shape=[shape] * parts,
        in_specs=[SMEM, VMEM],
        out_specs=[VMEM] * parts,
        scratch_shapes=[pltpu.VMEM((channels, total), BF16)],
        compiler_params=PARAMS,
    )(low, patch)


def gradient_kernel(pieces, place, *refs):
    cots, patches = refs[:2], refs[2 : 2 + pieces]
    out, cot, pat, win = refs[2 + pieces :]
    rows, size = cots[0].shape[0], patches[0].shape[0]
    chans = pieces * size
    core, x = place[0], place[1]
    plane = HEIGHT * WIDTH
    for index, ref in enumerate(cots):
        start = pl.multiple_of(jnp.bitwise_xor(core, index) * rows, 16)
        for i in range(DEPTH):
            cot[pl.ds(start, rows), SPAN * i : SPAN * i + plane] = ref[:, plane * i : plane * (i + 1)]
            cot[pl.ds(start, rows), SPAN * i + plane : SPAN * (i + 1)] = jnp.zeros((rows, SPAN - plane), BF16)
    for index, ref in enumerate(patches):
        start = pl.multiple_of(jnp.bitwise_xor(x, index) * size, 16)
        pat[pl.ds(start, size), :] = ref[...]

    main = PLANES * SPAN
    lane = lax.broadcasted_iota(jnp.int32, (chans, LANES), 1) % WIDTH
    last, before = lane == WIDTH - 1, lane == WIDTH - 2
    first_tail, second_tail = pat[:, main : main + LANES], pat[:, main + LANES :]

    def window(b, e):
        start = (KERNEL * b + e) * chans
        return slice(start, start + chans)

    for q in range(main // LANES):
        here = slice(LANES * q, LANES * (q + 1))
        block = pat[:, here]
        to_last, to_before = (WIDTH - 1 - q) % LANES, (WIDTH - 2 - q) % LANES
        win[window(0, 0), here] = block
        win[window(0, 1), here] = jnp.where(
            last, pltpu.roll(first_tail, to_last, 1), pltpu.roll(block, LANES - 1, 1)
        )
        win[window(0, 2), here] = jnp.where(
            last,
            pltpu.roll(second_tail, to_last, 1),
            jnp.where(before, pltpu.roll(first_tail, to_before, 1), pltpu.roll(block, LANES - 2, 1)),
        )
    for e in range(KERNEL):
        for b in range(1, KERNEL):
            shift = WIDTH * b
            win[window(b, e), : main - shift] = win[window(0, e), shift:]
            win[window(b, e), main - shift :] = jnp.zeros((chans, shift), BF16)
    for a in range(KERNEL):
        out[a] = lax.dot_general(
            cot[...],
            win[:, SPAN * a : SPAN * (a + DEPTH)],
            (((1,), (1,)), ((), ())),
            preferred_element_type=F32,
        )


def gradient_block(place, own_cots, other_cots, slot, patches):
    _, rows, vox = own_cots.shape
    size, total = patches[0].shape
    pieces = len(patches)
    chans = pieces * size
    taps = KERNEL * KERNEL
    half = pl.BlockSpec((None, rows, vox), lambda i: (slot, 0, 0))
    piece = pl.BlockSpec((size, total), lambda i: (0, 0))
    return pl.pallas_call(
        lambda *refs: gradient_kernel(pieces, *refs),
        grid=(1,),
        out_shape=jax.ShapeDtypeStruct((KERNEL, 2 * rows, taps * chans), F32),
        in_specs=[SMEM, half, half] + [piece] * pieces,
        out_specs=pl.BlockSpec((KERNEL, 2 * rows, taps * chans), lambda i: (0, 0, 0)),
        scratch_shapes=[
            pltpu.VMEM((2 * rows, DEPTH * SPAN), BF16),
            pltpu.VMEM((chans, total), BF16),
            pltpu.VMEM((taps * chans, PLANES * SPAN), BF16),
        ],
        compiler_params=PARAMS,
    )(place, own_cots, other_cots, *patches)


def gram_kernel(rep, *refs):
    grads, out = refs[:-1], refs[-1]
    count = len(grads)
    step, rows, lanes = grads[0].shape
    group = min(count, 8)

    @pl.when(pl.program_id(0) == 0)
    def _():
        out[...] = jnp.zeros_like(out)

    lane = lax.broadcasted_iota(jnp.int32, (1, LANES), 1)
    for first in range(0, count, group):
        for second in range(0, first + 1, group):
            pairs = [
                (i, j)
                for i in range(first, first + group)
                for j in range(second, min(second + group, i + 1))
            ]

            def body(r, sums):
                start = pl.multiple_of(r * 8, 8)
                sums = list(sums)
                for left in range(0, lanes, LANES):
                    width = min(LANES, lanes - left)
                    need = sorted({i for pair in pairs for i in pair})
                    tile = {i: grads[i][0, pl.ds(start, 8), left : left + width] for i in need}
                    for n, (i, j) in enumerate(pairs):
                        product = tile[i] * tile[j]
                        if width < LANES:
                            product = jnp.pad(product, ((0, 0), (0, LANES - width)))
                        sums[n] = sums[n] + product
                return tuple(sums)

            zero = jnp.zeros((8, LANES), F32)
            sums = lax.fori_loop(0, rows // 8, body, (zero,) * len(pairs))
            for (i, j), value in zip(pairs, sums):
                total = jnp.sum(value)
                a, b = jnp.bitwise_xor(rep[0], i), jnp.bitwise_xor(rep[0], j)
                for at in [a * count + b, b * count + a][: 1 + (i != j)]:
                    out[pl.ds(at // LANES, 1), :] += jnp.where(lane == at % LANES, total, 0.0)


def gram_partial(rep, grads):
    count = len(grads)
    step, rows, lanes = grads[0].shape
    out_rows = -(-count * count // LANES)
    return pl.pallas_call(
        gram_kernel,
        grid=(step,),
        out_shape=jax.ShapeDtypeStruct((out_rows, LANES), F32),
        in_specs=[SMEM] + [pl.BlockSpec((1, rows, lanes), lambda i: (i, 0, 0))] * count,
        out_specs=pl.BlockSpec((out_rows, LANES), lambda i: (0, 0)),
        compiler_params=PARAMS,
    )(rep, *grads)


def tree_weights(gram, count):
    def inner(left, right):
        total = 0.0
        for i, u in left.items():
            part = 0.0
            for j, v in right.items():
                part = part + v * gram(i, j)
            total = total + u * part
        return total

    def combine(low, level):
        if 2**level == count:
            return {low: jnp.ones((1, LANES), F32)}
        former, latter = combine(low, level + 1), combine(low + 2**level, level + 1)
        dot = inner(former, latter)
        scale_former = 1.0 - dot / (2.0 * inner(former, former))
        scale_latter = 1.0 - dot / (2.0 * inner(latter, latter))
        joined = {i: scale_former * u for i, u in former.items()}
        joined.update({i: scale_latter * v for i, v in latter.items()})
        return joined

    return combine(0, 0)


def combine_kernel(count, place, gram, *refs):
    grads, outs, factors = refs[:count], refs[count:-1], refs[-1]
    step = pl.program_id(0)

    @pl.when(step == 0)
    def _():
        weights = tree_weights(lambda i, j: jnp.full((1, LANES), gram[i * count + j]), count)
        for i, value in weights.items():
            factors[i : i + 1, :] = value

    scales = [factors[pl.ds(jnp.bitwise_xor(place[0], i), 1), :][:, :1] for i in range(count)]
    for index, out in enumerate(outs):

        @pl.when(step == index)
        def _():
            for a in range(KERNEL):
                total = scales[0] * grads[0][a, 0]
                for scale, grad in zip(scales[1:], grads[1:]):
                    total = total + scale * grad[a, 0]
                out[a] = total


def combine_blocks(place, gram, grads, blocks):
    count = len(grads)
    step, rows, lanes = grads[0].shape
    grads = [grad.reshape(step, blocks, rows // blocks, lanes) for grad in grads]
    half = blocks // 2

    def index(i, place):
        core = jnp.bitwise_xor(i // half, place[1])
        low = jnp.bitwise_xor(i % half, place[2])
        return (0, core * half + low, 0, 0)

    block = pl.BlockSpec((step, 1, rows // blocks, lanes), index)
    out_shape = (step, rows // blocks, lanes)
    return pl.pallas_call(
        lambda *refs: combine_kernel(count, *refs),
        grid_spec=pltpu.PrefetchScalarGridSpec(
            num_scalar_prefetch=1,
            grid=(blocks,),
            in_specs=[SMEM] + [block] * count,
            out_specs=[pl.BlockSpec(out_shape, lambda i, place: (0, 0, 0))] * blocks,
            scratch_shapes=[pltpu.VMEM((count, LANES), F32)],
        ),
        out_shape=[jax.ShapeDtypeStruct(out_shape, F32)] * blocks,
        compiler_params=PARAMS,
    )(place, gram, *grads)


def update_kernel(parts, pieces, place, weight, momentum, *refs):
    blocks, (new_weight, new_momentum, buf) = refs[:-3], refs[-3:]
    taps = KERNEL * KERNEL
    per_tap = blocks[0].shape[2] // taps
    size = weight.shape[2] // (2 * parts * pieces)
    for index, ref in enumerate(blocks):
        core = jnp.bitwise_xor(index // parts, place[1])
        low = jnp.bitwise_xor(index % parts, place[2])
        buf[core * parts + low] = ref[...]
    for t in range(KERNEL * taps):
        a, rest = t // taps, t % taps
        line = []
        for x in range(pieces):
            left = rest * per_tap + x * (per_tap // pieces)
            for source in range(2 * parts):
                line.append(buf[source, a, :, left : left + size])
        combined = jnp.concatenate(line, axis=1)
        updated = momentum_decay * momentum[:, t, :] + combined
        new_momentum[:, t, :] = updated
        new_weight[:, t, :] = weight[:, t, :] - learning_rate * updated


def update(place, weight, momentum, blocks, parts, pieces):
    shape = jax.ShapeDtypeStruct(weight.shape, F32)
    return pl.pallas_call(
        lambda *refs: update_kernel(parts, pieces, *refs),
        out_shape=[shape, shape],
        in_specs=[SMEM] + [VMEM] * (2 + len(blocks)),
        out_specs=[VMEM, VMEM],
        scratch_shapes=[pltpu.VMEM((len(blocks),) + blocks[0].shape, F32)],
        compiler_params=PARAMS,
    )(place, weight, momentum, *blocks)


def shards(patches, cotangents, weight, momentum):
    replicas, columns = lax.axis_size("rep"), lax.axis_size("ch")
    parts, pieces = replicas // 2, columns // 2
    rep, ch = lax.axis_index("rep"), lax.axis_index("ch")
    upper, low = rep // parts, rep % parts
    core, x = ch % 2, ch // 2
    patch, cot = patches[0], cotangents[0]
    rows = cot.shape[0] // 2

    kept = lax.dynamic_slice_in_dim(cot, upper * rows, rows)
    sent = lax.dynamic_slice_in_dim(cot, (1 - upper) * rows, rows)
    cots = {0: jnp.stack([kept, swap(sent, "rep", parts)])}
    bit = parts // 2
    while bit:
        cots.update({mask | bit: swap(value, "rep", bit) for mask, value in cots.items()})
        bit //= 2
    other_cots = {mask: swap(value, "ch", 1) for mask, value in cots.items()}

    packed = pack_patch(low[None], patch, parts)
    place = jnp.stack([core, x])
    grads = []
    for mask in range(replicas):
        part, slot = mask % parts, mask // parts
        mine = swap(packed[part], "rep", mask) if mask else packed[part]
        spread = [mine] + [swap(mine, "ch", 2 * other) for other in range(1, pieces)]
        grads.append(gradient_block(place, cots[part], other_cots[part], slot, spread))

    gram = gram_partial(rep[None], grads)
    devices = replicas * columns
    every = jnp.broadcast_to(gram, (devices,) + gram.shape)
    gram = lax.all_to_all(every, ("rep", "ch"), 0, 0, tiled=True).sum(0).reshape(-1)
    blocks = combine_blocks(jnp.stack([rep, core, low]), gram, grads, 2 * parts)
    blocks = [
        swap_both(block, index % parts, index // parts) if index else block
        for index, block in enumerate(blocks)
    ]
    return tuple(update(jnp.stack([rep, core, low]), weight, momentum, blocks, parts, pieces))


def solution(mesh):
    in_specs = (
        P("rep", "ch", None),
        P("rep", "ch", None),
        P(("ch", "rep"), None, None),
        P(("ch", "rep"), None, None),
    )
    out_specs = (P(("ch", "rep"), None, None), P(("ch", "rep"), None, None))
    return jax.shard_map(shards, mesh=mesh, in_specs=in_specs, out_specs=out_specs, check_vma=False)
```

```python
import jax
import jax.numpy as jnp
from jax import lax
from jax.experimental import pallas as pl
from jax.experimental.pallas import tpu as pltpu
from jax.sharding import Mesh
from jax.sharding import PartitionSpec as P

KERNEL = 3
DEPTH = 6
HEIGHT = 14
WIDTH = 32
ROWS = HEIGHT + KERNEL - 1
CELLS = WIDTH + KERNEL - 1
PLANES = DEPTH + KERNEL - 1
SPAN = ROWS * WIDTH
LANES = 128
PER_VREG = LANES // WIDTH

momentum_decay = 0.9
learning_rate = 0.05

BF16 = jnp.bfloat16
F32 = jnp.float32
VMEM = pl.BlockSpec(memory_space=pltpu.VMEM)
SMEM = pl.BlockSpec(memory_space=pltpu.SMEM)
PARAMS = pltpu.CompilerParams(vmem_limit_bytes=56 * 2**20)
SMALL = pltpu.CompilerParams(vmem_limit_bytes=20 * 2**20)


REP = ("half", "low")
CH = ("x", "core")


def swap(value, axes, mask):
    pairs = [(source, source ^ mask) for source in range(lax.axis_size(axes))]
    return lax.ppermute(value, axes, pairs)


def in_vmem(value):
    return pltpu.with_memory_space_constraint(value, pltpu.VMEM)


def hold_back(values, until):
    values, until = list(values), list(until)
    here = pl.BlockSpec(memory_space=pl.ANY)
    return pl.pallas_call(
        lambda *refs: None,
        out_shape=[jax.ShapeDtypeStruct(value.shape, value.dtype) for value in values],
        in_specs=[here] * (len(values) + len(until)),
        out_specs=[here] * len(values),
        input_output_aliases={index: index for index in range(len(values))},
        compiler_params=pltpu.CompilerParams(vmem_limit_bytes=2**20),
    )(*values, *until)


def pack_kernel(low, patch_ref, *refs):
    parts, buf = refs[:-1], refs[-1]
    main = PLANES * SPAN
    for row in range(PLANES * ROWS):
        buf[:, WIDTH * row : WIDTH * (row + 1)] = patch_ref[:, CELLS * row : CELLS * row + WIDTH]
    total = PLANES * ROWS * CELLS
    tail = 2 * LANES
    k = lax.broadcasted_iota(jnp.int32, (total, tail), 0)
    n = lax.broadcasted_iota(jnp.int32, (total, tail), 1)
    lane = n % LANES
    row = PER_VREG * (lane % WIDTH) + lane // WIDTH
    pick = (k == row * CELLS + WIDTH + n // LANES).astype(BF16)
    buf[:, main:] = jnp.dot(patch_ref[...], pick, preferred_element_type=F32).astype(BF16)
    size = parts[0].shape[1]
    for mask, out in enumerate(parts):
        start = pl.multiple_of(jnp.bitwise_xor(low[0], mask) * size, 16)
        out[0] = buf[pl.ds(start, size), :]


def pack_patch(low, patch, parts):
    size = -(-patch.shape[0] // (16 * parts)) * 16
    if size * parts != patch.shape[0]:
        by_part = patch.reshape(parts, -1, patch.shape[1])
        by_part = jnp.pad(by_part, ((0, 0), (0, size - by_part.shape[1]), (0, 0)))
        patch = by_part.reshape(parts * size, -1)
    channels, total = patch.shape
    shape = jax.ShapeDtypeStruct((1, channels // parts, total), BF16)
    return pl.pallas_call(
        pack_kernel,
        out_shape=[shape] * parts,
        in_specs=[SMEM, VMEM],
        out_specs=[VMEM] * parts,
        scratch_shapes=[pltpu.VMEM((channels, total), BF16)],
        compiler_params=SMALL,
    )(low, patch)


def write_windows(pat, win, chans, start):
    size = pat.shape[0]
    main = PLANES * SPAN
    lane = lax.broadcasted_iota(jnp.int32, (size, LANES), 1) % WIDTH
    last, before = lane == WIDTH - 1, lane == WIDTH - 2
    first_tail, second_tail = pat[:, main : main + LANES], pat[:, main + LANES :]

    def window(b, e):
        return pl.ds((KERNEL * b + e) * chans + start, size)

    for q in range(main // LANES):
        here = slice(LANES * q, LANES * (q + 1))
        block = pat[:, here]
        to_last, to_before = (WIDTH - 1 - q) % LANES, (WIDTH - 2 - q) % LANES
        win[window(0, 0), here] = block
        win[window(0, 1), here] = jnp.where(
            last, pltpu.roll(first_tail, to_last, 1), pltpu.roll(block, LANES - 1, 1)
        )
        win[window(0, 2), here] = jnp.where(
            last,
            pltpu.roll(second_tail, to_last, 1),
            jnp.where(before, pltpu.roll(first_tail, to_before, 1), pltpu.roll(block, LANES - 2, 1)),
        )
    for e in range(KERNEL):
        for b in range(1, KERNEL):
            shift = WIDTH * b
            win[window(b, e), : main - shift] = win[window(0, e), shift:]
            win[window(b, e), main - shift :] = jnp.zeros((size, shift), BF16)


def gradient_kernel(pieces, place, *refs):
    cots, patches = refs[:2], refs[2 : 2 + pieces]
    out, cot, pat, win = refs[2 + pieces :]
    rows, size = cots[0].shape[0], patches[0].shape[0]
    chans = pieces * size
    core, x = place[0], place[1]
    plane = HEIGHT * WIDTH
    for index, ref in enumerate(cots):
        start = pl.multiple_of(jnp.bitwise_xor(core, index) * rows, 16)
        for i in range(DEPTH):
            cot[pl.ds(start, rows), SPAN * i : SPAN * i + plane] = ref[:, plane * i : plane * (i + 1)]
            cot[pl.ds(start, rows), SPAN * i + plane : SPAN * (i + 1)] = jnp.zeros((rows, SPAN - plane), BF16)
    for index, ref in enumerate(patches):
        start = pl.multiple_of(jnp.bitwise_xor(x, index) * size, 16)
        pat[pl.ds(start, size), :] = ref[...]

    write_windows(pat, win, chans, 0)
    for a in range(KERNEL):
        out[a] = lax.dot_general(
            cot[...],
            win[:, SPAN * a : SPAN * (a + DEPTH)],
            (((1,), (1,)), ((), ())),
            preferred_element_type=F32,
        )


def gradient_block(place, cots, patches):
    _, rows, vox = cots[0][0].shape
    _, size, total = patches[0][0].shape
    chans = len(patches) * size
    taps = KERNEL * KERNEL

    def part(array, slot):
        return pl.BlockSpec((None,) + array.shape[1:], lambda i: (slot, 0, 0))

    operands = [*cots, *patches]
    return pl.pallas_call(
        lambda *refs: gradient_kernel(len(patches), *refs),
        grid=(1,),
        out_shape=jax.ShapeDtypeStruct((KERNEL, 2 * rows, taps * chans), F32),
        in_specs=[SMEM] + [part(*operand) for operand in operands],
        out_specs=pl.BlockSpec((KERNEL, 2 * rows, taps * chans), lambda i: (0, 0, 0)),
        scratch_shapes=[
            pltpu.VMEM((2 * rows, DEPTH * SPAN), BF16),
            pltpu.VMEM((chans, total), BF16),
            pltpu.VMEM((taps * chans, PLANES * SPAN), BF16),
        ],
        compiler_params=PARAMS,
    )(place, *[array for array, _ in operands])


def gram_kernel(rep, *refs):
    grads, out = refs[:-1], refs[-1]
    count = len(grads)
    step, rows, lanes = grads[0].shape
    group = min(count, 8)

    @pl.when(pl.program_id(0) == 0)
    def _():
        out[...] = jnp.zeros_like(out)

    lane = lax.broadcasted_iota(jnp.int32, (1, LANES), 1)
    for first in range(0, count, group):
        for second in range(0, first + 1, group):
            pairs = [
                (i, j)
                for i in range(first, first + group)
                for j in range(second, min(second + group, i + 1))
            ]

            def body(r, sums):
                start = pl.multiple_of(r * 8, 8)
                sums = list(sums)
                for left in range(0, lanes, LANES):
                    width = min(LANES, lanes - left)
                    need = sorted({i for pair in pairs for i in pair})
                    tile = {i: grads[i][0, pl.ds(start, 8), left : left + width] for i in need}
                    for n, (i, j) in enumerate(pairs):
                        product = tile[i] * tile[j]
                        if width < LANES:
                            product = jnp.pad(product, ((0, 0), (0, LANES - width)))
                        sums[n] = sums[n] + product
                return tuple(sums)

            zero = jnp.zeros((8, LANES), F32)
            sums = lax.fori_loop(0, rows // 8, body, (zero,) * len(pairs))
            for (i, j), value in zip(pairs, sums):
                total = jnp.sum(value)
                a, b = jnp.bitwise_xor(rep[0], i), jnp.bitwise_xor(rep[0], j)
                for at in [a * count + b, b * count + a][: 1 + (i != j)]:
                    out[pl.ds(at // LANES, 1), :] += jnp.where(lane == at % LANES, total, 0.0)


def gram_partial(rep, grads):
    count = len(grads)
    step, rows, lanes = grads[0].shape
    out_rows = -(-count * count // LANES)
    return pl.pallas_call(
        gram_kernel,
        grid=(step,),
        out_shape=jax.ShapeDtypeStruct((out_rows, LANES), F32),
        in_specs=[SMEM] + [pl.BlockSpec((1, rows, lanes), lambda i: (i, 0, 0))] * count,
        out_specs=pl.BlockSpec((out_rows, LANES), lambda i: (0, 0)),
        compiler_params=PARAMS,
    )(rep, *grads)


def tree_weights(gram, count):
    def inner(left, right):
        total = 0.0
        for i, u in left.items():
            part = 0.0
            for j, v in right.items():
                part = part + v * gram(i, j)
            total = total + u * part
        return total

    def combine(low, level):
        if 2**level == count:
            return {low: jnp.ones((1, LANES), F32)}
        former, latter = combine(low, level + 1), combine(low + 2**level, level + 1)
        dot = inner(former, latter)
        scale_former = 1.0 - dot / (2.0 * inner(former, former))
        scale_latter = 1.0 - dot / (2.0 * inner(latter, latter))
        joined = {i: scale_former * u for i, u in former.items()}
        joined.update({i: scale_latter * v for i, v in latter.items()})
        return joined

    return combine(0, 0)


def combine_kernel(count, place, gram, *refs):
    grads, outs, factors = refs[:count], refs[count:-1], refs[-1]
    step = pl.program_id(0)

    @pl.when(step == 0)
    def _():
        weights = tree_weights(lambda i, j: jnp.full((1, LANES), gram[i * count + j]), count)
        for i, value in weights.items():
            factors[i : i + 1, :] = value

    scales = [factors[pl.ds(jnp.bitwise_xor(place[0], i), 1), :][:, :1] for i in range(count)]
    for index, out in enumerate(outs):

        @pl.when(step == index)
        def _():
            for a in range(KERNEL):
                total = scales[0] * grads[0][a, 0]
                for scale, grad in zip(scales[1:], grads[1:]):
                    total = total + scale * grad[a, 0]
                out[a] = total


def combine_blocks(place, gram, grads, blocks):
    count = len(grads)
    step, rows, lanes = grads[0].shape
    grads = [grad.reshape(step, blocks, rows // blocks, lanes) for grad in grads]
    half = blocks // 2

    def index(i, place):
        core = jnp.bitwise_xor(i // half, place[1])
        low = jnp.bitwise_xor(i % half, place[3])
        return (0, core * half + low, 0, 0)

    block = pl.BlockSpec((step, 1, rows // blocks, lanes), index)
    out_shape = (step, rows // blocks, lanes)
    return pl.pallas_call(
        lambda *refs: combine_kernel(count, *refs),
        grid_spec=pltpu.PrefetchScalarGridSpec(
            num_scalar_prefetch=1,
            grid=(blocks,),
            in_specs=[SMEM] + [block] * count,
            out_specs=[pl.BlockSpec(out_shape, lambda i, place: (0, 0, 0))] * blocks,
            scratch_shapes=[pltpu.VMEM((count, LANES), F32)],
        ),
        out_shape=[jax.ShapeDtypeStruct(out_shape, F32)] * blocks,
        compiler_params=PARAMS,
    )(place, gram, *grads)


def update_kernel(parts, pieces, place, weight, momentum, *refs):
    blocks, (new_weight, new_momentum, buf) = refs[:-3], refs[-3:]
    taps = KERNEL * KERNEL
    per_tap = blocks[0].shape[2] // taps
    size = weight.shape[2] // (2 * parts * pieces)
    for index, ref in enumerate(blocks):
        core = jnp.bitwise_xor(index // parts, place[1])
        low = jnp.bitwise_xor(index % parts, place[3])
        buf[core * parts + low] = ref[0]
    for t in range(taps):
        line = []
        for x in range(pieces):
            left = t * per_tap + x * (per_tap // pieces)
            for source in range(2 * parts):
                line.append(buf[source, :, left : left + size])
        updated = momentum_decay * momentum[t] + jnp.concatenate(line, axis=1)
        new_momentum[t] = updated
        new_weight[t] = weight[t] - learning_rate * updated


def update(place, weight, momentum, blocks, parts, pieces):
    weight, momentum = jnp.swapaxes(weight, 0, 1), jnp.swapaxes(momentum, 0, 1)
    taps, rows, chans = weight.shape
    lanes = blocks[0].shape[2]
    shape = jax.ShapeDtypeStruct(weight.shape, F32)
    own = pl.BlockSpec((taps // KERNEL, rows, chans), lambda a: (a, 0, 0))
    block = pl.BlockSpec((1, rows, lanes), lambda a: (a, 0, 0))
    results = pl.pallas_call(
        lambda *refs: update_kernel(parts, pieces, *refs),
        grid=(KERNEL,),
        out_shape=[shape, shape],
        in_specs=[SMEM, own, own] + [block] * len(blocks),
        out_specs=[own, own],
        scratch_shapes=[pltpu.VMEM((len(blocks), rows, lanes), F32)],
        compiler_params=SMALL,
    )(place, weight, momentum, *blocks)
    return tuple(jnp.swapaxes(result, 0, 1) for result in results)


def staged_gradient_kernel(count, mask, masks, slots, place, *refs):
    pieces = len(slots) - 2
    sources, refs = refs[: len(slots)], refs[len(slots) :]
    others, refs = refs[: len(masks)], refs[len(masks) :]
    gram_in, out, kept, gram_out, cot, win, sems = refs
    rows, size = sources[0].shape[1], sources[2].shape[1]
    rep, core, x = place[0], place[1], place[2]

    cot[2 * rows :, :] = jnp.zeros((cot.shape[0] - 2 * rows, cot.shape[1]), BF16)
    plane = HEIGHT * WIDTH
    for index in range(2):
        here = pl.ds(pl.multiple_of(jnp.bitwise_xor(core, index) * rows, 16), rows)
        for i in range(DEPTH):
            left = SPAN * i
            cot[here, left : left + plane] = sources[index][slots[index], :, plane * i : plane * (i + 1)]
            cot[here, left + plane : left + SPAN] = jnp.zeros((rows, SPAN - plane), BF16)
    for turn in range(pieces):

        @pl.when(x == turn)
        def _():
            for index in range(pieces):
                start = (turn ^ index) * size
                write_windows(sources[2 + index].at[slots[2 + index]], win, pieces * size, start)

    stores = []
    for a in range(KERNEL):
        product = lax.dot_general(
            cot[...],
            win[:, SPAN * a : SPAN * (a + DEPTH)],
            (((1,), (1,)), ((), ())),
            preferred_element_type=F32,
        )
        out[a] = product[: 2 * rows]
        stores.append(pltpu.make_async_copy(out.at[a], kept.at[a], sems.at[a]))
        stores[-1].start()

    lanes = out.shape[2]
    full, rest = lanes // LANES * LANES, lanes % LANES

    def body(step, sums):
        start = pl.multiple_of(step * 8, 8)
        sums = [list(pair) for pair in sums]
        for a in range(KERNEL):
            for left in range(0, full, LANES):
                mine = out[a, pl.ds(start, 8), left : left + LANES]
                for pair, ref in zip(sums, (*others, None)):
                    other = mine if ref is None else ref[a, pl.ds(start, 8), left : left + LANES]
                    pair[0] = pair[0] + mine * other
            if rest:
                mine = out[a, pl.ds(start, 8), full:]
                for pair, ref in zip(sums, (*others, None)):
                    other = mine if ref is None else ref[a, pl.ds(start, 8), full:]
                    pair[1] = pair[1] + mine * other
        return tuple(tuple(pair) for pair in sums)

    zero = (jnp.zeros((8, LANES), F32), jnp.zeros((8, max(rest, 1)), F32))
    sums = lax.fori_loop(0, 2 * rows // 8, body, (zero,) * (len(others) + 1))
    lane = lax.broadcasted_iota(jnp.int32, (1, LANES), 1)
    line = gram_in[...]
    first = jnp.bitwise_xor(rep, mask)
    for other, pair in zip((*masks, mask), sums):
        total = jnp.sum(pair[0]) + jnp.sum(pair[1])
        second = jnp.bitwise_xor(rep, other)
        here = (lane == first * count + second) | (lane == second * count + first)
        line = line + jnp.where(here, total, 0.0)
    gram_out[...] = jnp.broadcast_to(line, gram_out.shape)
    for store in stores:
        store.wait()


def staged_gradient(count, place, mask, cots, patches, before, gram, copies=None):
    _, rows, vox = cots[0][0].shape
    _, size, total = patches[0][0].shape
    chans = len(patches) * size
    taps = KERNEL * KERNEL
    operands = [*cots, *patches]
    shape = (KERNEL, 2 * rows, taps * chans)
    line = (1, LANES) if copies is None else (copies, 1, LANES)
    far = pl.BlockSpec(memory_space=pl.ANY)
    slots = [slot for _, slot in operands]
    return pl.pallas_call(
        lambda *refs: staged_gradient_kernel(count, mask, list(before), slots, *refs),
        out_shape=[pltpu.VMEM(shape, F32), pltpu.HBM(shape, F32), jax.ShapeDtypeStruct(line, F32)],
        in_specs=[SMEM] + [VMEM] * (len(operands) + len(before) + 1),
        out_specs=[VMEM, far, VMEM],
        scratch_shapes=[
            pltpu.VMEM((-(-2 * rows // 256) * 256, DEPTH * SPAN), BF16),
            pltpu.VMEM((taps * chans, PLANES * SPAN), BF16),
            pltpu.SemaphoreType.DMA((KERNEL,)),
        ],
        compiler_params=pltpu.CompilerParams(vmem_limit_bytes=14 * 2**20),
    )(place, *[in_vmem(array) for array, _ in operands], *[in_vmem(value) for value in before.values()], gram)


def staged_combine_kernel(count, place, gram, *refs):
    grads, outs = refs[:count], refs[count:-3]
    stage, factors, sems = refs[-3:]
    rows = outs[0].shape[1]
    half = len(outs) // 2
    copies = [
        [pltpu.make_async_copy(grad.at[a], stage.at[i, a], sems.at[i, a]) for i, grad in enumerate(grads)]
        for a in range(KERNEL)
    ]
    for group in copies:
        for copy in group:
            copy.start()
    total = gram[0]
    for device in range(1, gram.shape[0]):
        total = total + gram[device]
    products = lambda i, j: jnp.broadcast_to(total[:, i * count + j : i * count + j + 1], (1, LANES))
    for i, value in tree_weights(products, count).items():
        factors[i : i + 1, :] = value
    scales = [factors[pl.ds(jnp.bitwise_xor(place[0], i), 1), :][:, :1] for i in range(count)]
    for a in range(KERNEL):
        for copy in copies[a]:
            copy.wait()
        for index, out in enumerate(outs):
            core = jnp.bitwise_xor(index // half, place[1])
            low = jnp.bitwise_xor(index % half, place[3])
            here = pl.ds(pl.multiple_of((core * half + low) * rows, 8), rows)
            sums = scales[0] * stage[0, a, here, :]
            for i in range(1, count):
                sums = sums + scales[i] * stage[i, a, here, :]
            out[a] = sums


def staged_combine(place, gram, grads, blocks):
    step, rows, lanes = grads[0].shape
    shape = (step, rows // blocks, lanes)
    return pl.pallas_call(
        lambda *refs: staged_combine_kernel(len(grads), *refs),
        out_shape=[jax.ShapeDtypeStruct(shape, F32)] * blocks,
        in_specs=[SMEM, VMEM] + [pl.BlockSpec(memory_space=pl.ANY)] * len(grads),
        out_specs=[VMEM] * blocks,
        scratch_shapes=[
            pltpu.VMEM((len(grads),) + grads[0].shape, F32),
            pltpu.VMEM((len(grads), LANES), F32),
            pltpu.SemaphoreType.DMA((len(grads), step)),
        ],
        compiler_params=pltpu.CompilerParams(vmem_limit_bytes=30 * 2**20),
    )(place, gram, *[pltpu.with_memory_space_constraint(grad, pltpu.HBM) for grad in grads])


def staged_blocks(place, low, patch, kept, sent):
    count = lax.axis_size(REP)
    devices = count * lax.axis_size(CH)
    along = lambda value, mask: swap(value, REP, mask)
    across = lambda value: swap(value, "x", 1)
    core = lambda value: swap(value, "core", 1)
    join = lambda *values: jnp.concatenate(values)
    near, grads, gram = {}, {}, jnp.zeros((1, LANES), F32)

    def add(mask, cot, other, patch, far, other_slot=0, far_slot=0, copies=None):
        nonlocal gram
        operands = [(cot, 0), (other, other_slot)], [(patch, 0), (far, far_slot)]
        near[mask], grads[mask], gram = staged_gradient(
            count, place, mask, *operands, near, gram, copies
        )

    cot0 = kept[None]
    cot4 = along(sent[None], 4)
    cot2 = along(cot0, 2)
    cot1 = along(cot0, 1)
    core0 = core(cot0)
    part0, part1, part2, part3 = pack_patch(low[None], patch, 4)
    part0, part1, core0 = hold_back([part0, part1, core0], [])
    far0 = across(part0)
    patch1 = along(part1, 1)

    part0, far0, patch1, cot1, cot2, cot4, part2 = hold_back(
        [part0, far0, patch1, cot1, cot2, cot4, part2], []
    )
    patch4 = along(part0, 4)
    far1 = across(patch1)
    core1 = core(cot1)
    cot3 = along(cot2, 1)
    patch2 = along(part2, 2)
    add(0, cot0, core0, part0, far0)

    part1, patch4, far1, core1, cot3, patch2 = hold_back([part1, patch4, far1, core1, cot3, patch2], [gram])
    patch5 = along(part1, 5)
    far42 = across(join(patch4, patch2))
    cot6 = along(cot4, 2)
    cot5 = along(cot4, 1)
    core42 = core(join(cot4, cot2))
    add(1, cot1, core1, patch1, far1)

    part2, patch5, far42, cot6, cot5, core42, part3 = hold_back(
        [part2, patch5, far42, cot6, cot5, core42, part3], [gram]
    )
    patch6 = along(part2, 6)
    far5 = across(patch5)
    cot7 = along(cot6, 1)
    patch3 = along(part3, 3)
    core53 = core(join(cot5, cot3))
    add(4, cot4, core42, patch4, far42)
    add(2, cot2, core42, patch2, far42, 1, 1)

    part3, patch6, far5, cot7, patch3, core53 = hold_back([part3, patch6, far5, cot7, patch3, core53], [gram])
    patch7 = along(part3, 7)
    far63 = across(join(patch6, patch3))
    core67 = core(join(cot6, cot7))
    add(5, cot5, core53, patch5, far5)

    patch7, far63, core67 = hold_back([patch7, far63, core67], [gram])
    far7 = across(patch7)
    add(3, cot3, core53, patch3, far63, 1, 1)
    add(6, cot6, core67, patch6, far63)
    (far7,) = hold_back([far7], [gram])
    add(7, cot7, core67, patch7, far7, 1, 0, devices)

    gram = lax.all_to_all(gram, REP + CH, 0, 0, tiled=True)
    return staged_combine(place, gram, [grads[mask] for mask in range(count)], count)


def plain_gradients(place, low, patch, kept, sent):
    replicas, columns = lax.axis_size(REP), lax.axis_size(CH)
    parts, pieces = replicas // 2, columns // 2
    cots = {0: jnp.stack([kept, swap(sent, "half", 1)])}
    bit = parts // 2
    while bit:
        cots.update({mask | bit: swap(value, "low", bit) for mask, value in cots.items()})
        bit //= 2
    other_cots = {mask: swap(value, "core", 1) for mask, value in cots.items()}
    packed = pack_patch(low[None], patch, parts)
    grads = []
    for mask in range(replicas):
        part, slot = mask % parts, mask // parts
        mine = swap(packed[part], REP, mask) if mask else packed[part]
        spread = [mine] + [swap(mine, "x", other) for other in range(1, pieces)]
        grads.append(
            gradient_block(
                place, [(cots[part], slot), (other_cots[part], slot)], [(value, 0) for value in spread]
            )
        )
    return grads


def plain_blocks(place, low, patch, kept, sent):
    replicas, columns = lax.axis_size(REP), lax.axis_size(CH)
    grads = plain_gradients(place[1:3], low, patch, kept, sent)
    gram = gram_partial(place[:1], grads)
    devices = replicas * columns
    every = jnp.broadcast_to(gram, (devices,) + gram.shape)
    gram = lax.all_to_all(every, REP + CH, 0, 0, tiled=True).sum(0).reshape(-1)
    return combine_blocks(place, gram, grads, replicas)


def shards(patches, cotangents, weight, momentum):
    replicas, columns = lax.axis_size(REP), lax.axis_size(CH)
    parts, pieces = replicas // 2, columns // 2
    rep, upper, low = lax.axis_index(REP), lax.axis_index("half"), lax.axis_index("low")
    place = jnp.stack([rep, lax.axis_index("core"), lax.axis_index("x"), low])
    patch, cot = patches[0], cotangents[0]
    rows = cot.shape[0] // 2

    kept = lax.dynamic_slice_in_dim(cot, upper * rows, rows)
    sent = lax.dynamic_slice_in_dim(cot, (1 - upper) * rows, rows)
    result = staged_blocks if (replicas, columns) == (8, 4) else plain_blocks
    blocks = result(place, low, patch, kept, sent)
    blocks = [
        swap(block, ("low", "core"), index % parts * 2 + index // parts) if index else block
        for index, block in enumerate(blocks)
    ]
    return update(place, weight, momentum, blocks, parts, pieces)


def solution(mesh):
    replicas, columns = mesh.shape["rep"], mesh.shape["ch"]
    split = Mesh(mesh.devices.reshape(2, replicas // 2, columns // 2, 2), REP + CH)
    inputs, state = P(REP, CH, None), P(CH + REP, None, None)
    return jax.shard_map(
        shards, mesh=split, in_specs=(inputs, inputs, state, state), out_specs=(state, state), check_vma=False
    )
```

```python
import jax
import jax.numpy as jnp
from jax import lax
from jax.experimental import pallas as pl
from jax.experimental.pallas import tpu as pltpu
from jax.sharding import Mesh
from jax.sharding import PartitionSpec as P

KERNEL = 3
DEPTH = 6
HEIGHT = 14
WIDTH = 32
ROWS = HEIGHT + KERNEL - 1
CELLS = WIDTH + KERNEL - 1
PLANES = DEPTH + KERNEL - 1
SPAN = ROWS * WIDTH
LANES = 128
PER_VREG = LANES // WIDTH

momentum_decay = 0.9
learning_rate = 0.05

BF16 = jnp.bfloat16
F32 = jnp.float32
VMEM = pl.BlockSpec(memory_space=pltpu.VMEM)
SMEM = pl.BlockSpec(memory_space=pltpu.SMEM)
PARAMS = pltpu.CompilerParams(vmem_limit_bytes=56 * 2**20)
SMALL = pltpu.CompilerParams(vmem_limit_bytes=20 * 2**20)


REP = ("half", "low")
CH = ("x", "core")


def swap(value, axes, mask):
    pairs = [(source, source ^ mask) for source in range(lax.axis_size(axes))]
    return lax.ppermute(value, axes, pairs)


def in_vmem(value):
    return pltpu.with_memory_space_constraint(value, pltpu.VMEM)


def hold_back(values, until):
    values, until = list(values), list(until)
    here = pl.BlockSpec(memory_space=pl.ANY)
    return pl.pallas_call(
        lambda *refs: None,
        out_shape=[jax.ShapeDtypeStruct(value.shape, value.dtype) for value in values],
        in_specs=[here] * (len(values) + len(until)),
        out_specs=[here] * len(values),
        input_output_aliases={index: index for index in range(len(values))},
        compiler_params=pltpu.CompilerParams(vmem_limit_bytes=2**20),
    )(*values, *until)


def pack_kernel(low, patch_ref, *refs):
    parts, buf = refs[:-1], refs[-1]
    main = PLANES * SPAN
    for row in range(PLANES * ROWS):
        buf[:, WIDTH * row : WIDTH * (row + 1)] = patch_ref[:, CELLS * row : CELLS * row + WIDTH]
    total = PLANES * ROWS * CELLS
    tail = 2 * LANES
    k = lax.broadcasted_iota(jnp.int32, (total, tail), 0)
    n = lax.broadcasted_iota(jnp.int32, (total, tail), 1)
    lane = n % LANES
    row = PER_VREG * (lane % WIDTH) + lane // WIDTH
    pick = (k == row * CELLS + WIDTH + n // LANES).astype(BF16)
    buf[:, main:] = jnp.dot(patch_ref[...], pick, preferred_element_type=F32).astype(BF16)
    size = parts[0].shape[1]
    for mask, out in enumerate(parts):
        start = pl.multiple_of(jnp.bitwise_xor(low[0], mask) * size, 16)
        out[0] = buf[pl.ds(start, size), :]


def pack_patch(low, patch, parts):
    size = -(-patch.shape[0] // (16 * parts)) * 16
    if size * parts != patch.shape[0]:
        by_part = patch.reshape(parts, -1, patch.shape[1])
        by_part = jnp.pad(by_part, ((0, 0), (0, size - by_part.shape[1]), (0, 0)))
        patch = by_part.reshape(parts * size, -1)
    channels, total = patch.shape
    shape = jax.ShapeDtypeStruct((1, channels // parts, total), BF16)
    return pl.pallas_call(
        pack_kernel,
        out_shape=[shape] * parts,
        in_specs=[SMEM, VMEM],
        out_specs=[VMEM] * parts,
        scratch_shapes=[pltpu.VMEM((channels, total), BF16)],
        compiler_params=SMALL,
    )(low, patch)


def write_windows(pat, win, chans, start):
    size = pat.shape[0]
    main = PLANES * SPAN
    lane = lax.broadcasted_iota(jnp.int32, (size, LANES), 1) % WIDTH
    last, before = lane == WIDTH - 1, lane == WIDTH - 2
    first_tail, second_tail = pat[:, main : main + LANES], pat[:, main + LANES :]

    def window(b, e):
        return pl.ds((KERNEL * b + e) * chans + start, size)

    for q in range(main // LANES):
        here = slice(LANES * q, LANES * (q + 1))
        block = pat[:, here]
        to_last, to_before = (WIDTH - 1 - q) % LANES, (WIDTH - 2 - q) % LANES
        win[window(0, 0), here] = block
        win[window(0, 1), here] = jnp.where(
            last, pltpu.roll(first_tail, to_last, 1), pltpu.roll(block, LANES - 1, 1)
        )
        win[window(0, 2), here] = jnp.where(
            last,
            pltpu.roll(second_tail, to_last, 1),
            jnp.where(before, pltpu.roll(first_tail, to_before, 1), pltpu.roll(block, LANES - 2, 1)),
        )
    for e in range(KERNEL):
        for b in range(1, KERNEL):
            shift = WIDTH * b
            win[window(b, e), : main - shift] = win[window(0, e), shift:]
            win[window(b, e), main - shift :] = jnp.zeros((size, shift), BF16)


def gradient_kernel(pieces, place, *refs):
    cots, patches = refs[:2], refs[2 : 2 + pieces]
    out, cot, pat, win = refs[2 + pieces :]
    rows, size = cots[0].shape[0], patches[0].shape[0]
    chans = pieces * size
    core, x = place[0], place[1]
    plane = HEIGHT * WIDTH
    for index, ref in enumerate(cots):
        start = pl.multiple_of(jnp.bitwise_xor(core, index) * rows, 16)
        for i in range(DEPTH):
            cot[pl.ds(start, rows), SPAN * i : SPAN * i + plane] = ref[:, plane * i : plane * (i + 1)]
            cot[pl.ds(start, rows), SPAN * i + plane : SPAN * (i + 1)] = jnp.zeros((rows, SPAN - plane), BF16)
    for index, ref in enumerate(patches):
        start = pl.multiple_of(jnp.bitwise_xor(x, index) * size, 16)
        pat[pl.ds(start, size), :] = ref[...]

    write_windows(pat, win, chans, 0)
    for a in range(KERNEL):
        out[a] = lax.dot_general(
            cot[...],
            win[:, SPAN * a : SPAN * (a + DEPTH)],
            (((1,), (1,)), ((), ())),
            preferred_element_type=F32,
        )


def gradient_block(place, cots, patches):
    _, rows, vox = cots[0][0].shape
    _, size, total = patches[0][0].shape
    chans = len(patches) * size
    taps = KERNEL * KERNEL

    def part(array, slot):
        return pl.BlockSpec((None,) + array.shape[1:], lambda i: (slot, 0, 0))

    operands = [*cots, *patches]
    return pl.pallas_call(
        lambda *refs: gradient_kernel(len(patches), *refs),
        grid=(1,),
        out_shape=jax.ShapeDtypeStruct((KERNEL, 2 * rows, taps * chans), F32),
        in_specs=[SMEM] + [part(*operand) for operand in operands],
        out_specs=pl.BlockSpec((KERNEL, 2 * rows, taps * chans), lambda i: (0, 0, 0)),
        scratch_shapes=[
            pltpu.VMEM((2 * rows, DEPTH * SPAN), BF16),
            pltpu.VMEM((chans, total), BF16),
            pltpu.VMEM((taps * chans, PLANES * SPAN), BF16),
        ],
        compiler_params=PARAMS,
    )(place, *[array for array, _ in operands])


def gram_kernel(rep, *refs):
    grads, out = refs[:-1], refs[-1]
    count = len(grads)
    step, rows, lanes = grads[0].shape
    group = min(count, 8)

    @pl.when(pl.program_id(0) == 0)
    def _():
        out[...] = jnp.zeros_like(out)

    lane = lax.broadcasted_iota(jnp.int32, (1, LANES), 1)
    for first in range(0, count, group):
        for second in range(0, first + 1, group):
            pairs = [
                (i, j)
                for i in range(first, first + group)
                for j in range(second, min(second + group, i + 1))
            ]

            def body(r, sums):
                start = pl.multiple_of(r * 8, 8)
                sums = list(sums)
                for left in range(0, lanes, LANES):
                    width = min(LANES, lanes - left)
                    need = sorted({i for pair in pairs for i in pair})
                    tile = {i: grads[i][0, pl.ds(start, 8), left : left + width] for i in need}
                    for n, (i, j) in enumerate(pairs):
                        product = tile[i] * tile[j]
                        if width < LANES:
                            product = jnp.pad(product, ((0, 0), (0, LANES - width)))
                        sums[n] = sums[n] + product
                return tuple(sums)

            zero = jnp.zeros((8, LANES), F32)
            sums = lax.fori_loop(0, rows // 8, body, (zero,) * len(pairs))
            for (i, j), value in zip(pairs, sums):
                total = jnp.sum(value)
                a, b = jnp.bitwise_xor(rep[0], i), jnp.bitwise_xor(rep[0], j)
                for at in [a * count + b, b * count + a][: 1 + (i != j)]:
                    out[pl.ds(at // LANES, 1), :] += jnp.where(lane == at % LANES, total, 0.0)


def gram_partial(rep, grads):
    count = len(grads)
    step, rows, lanes = grads[0].shape
    out_rows = -(-count * count // LANES)
    return pl.pallas_call(
        gram_kernel,
        grid=(step,),
        out_shape=jax.ShapeDtypeStruct((out_rows, LANES), F32),
        in_specs=[SMEM] + [pl.BlockSpec((1, rows, lanes), lambda i: (i, 0, 0))] * count,
        out_specs=pl.BlockSpec((out_rows, LANES), lambda i: (0, 0)),
        compiler_params=PARAMS,
    )(rep, *grads)


def tree_weights(gram, count):
    def inner(left, right):
        total = 0.0
        for i, u in left.items():
            part = 0.0
            for j, v in right.items():
                part = part + v * gram(i, j)
            total = total + u * part
        return total

    def combine(low, level):
        if 2**level == count:
            return {low: jnp.ones((1, LANES), F32)}
        former, latter = combine(low, level + 1), combine(low + 2**level, level + 1)
        dot = inner(former, latter)
        scale_former = 1.0 - dot / (2.0 * inner(former, former))
        scale_latter = 1.0 - dot / (2.0 * inner(latter, latter))
        joined = {i: scale_former * u for i, u in former.items()}
        joined.update({i: scale_latter * v for i, v in latter.items()})
        return joined

    return combine(0, 0)


def combine_kernel(count, place, gram, *refs):
    grads, outs, factors = refs[:count], refs[count:-1], refs[-1]
    step = pl.program_id(0)

    @pl.when(step == 0)
    def _():
        weights = tree_weights(lambda i, j: jnp.full((1, LANES), gram[i * count + j]), count)
        for i, value in weights.items():
            factors[i : i + 1, :] = value

    scales = [factors[pl.ds(jnp.bitwise_xor(place[0], i), 1), :][:, :1] for i in range(count)]
    for index, out in enumerate(outs):

        @pl.when(step == index)
        def _():
            for a in range(KERNEL):
                total = scales[0] * grads[0][a, 0]
                for scale, grad in zip(scales[1:], grads[1:]):
                    total = total + scale * grad[a, 0]
                out[a] = total


def combine_blocks(place, gram, grads, blocks):
    count = len(grads)
    step, rows, lanes = grads[0].shape
    grads = [grad.reshape(step, blocks, rows // blocks, lanes) for grad in grads]
    half = blocks // 2

    def index(i, place):
        core = jnp.bitwise_xor(i // half, place[1])
        low = jnp.bitwise_xor(i % half, place[3])
        return (0, core * half + low, 0, 0)

    block = pl.BlockSpec((step, 1, rows // blocks, lanes), index)
    out_shape = (step, rows // blocks, lanes)
    return pl.pallas_call(
        lambda *refs: combine_kernel(count, *refs),
        grid_spec=pltpu.PrefetchScalarGridSpec(
            num_scalar_prefetch=1,
            grid=(blocks,),
            in_specs=[SMEM] + [block] * count,
            out_specs=[pl.BlockSpec(out_shape, lambda i, place: (0, 0, 0))] * blocks,
            scratch_shapes=[pltpu.VMEM((count, LANES), F32)],
        ),
        out_shape=[jax.ShapeDtypeStruct(out_shape, F32)] * blocks,
        compiler_params=PARAMS,
    )(place, gram, *grads)


def update_kernel(parts, pieces, place, weight, momentum, *refs):
    blocks, (new_weight, new_momentum, buf) = refs[:-3], refs[-3:]
    taps = KERNEL * KERNEL
    per_tap = blocks[0].shape[2] // taps
    size = weight.shape[2] // (2 * parts * pieces)
    for index, ref in enumerate(blocks):
        core = jnp.bitwise_xor(index // parts, place[1])
        low = jnp.bitwise_xor(index % parts, place[3])
        buf[core * parts + low] = ref[0]
    for t in range(taps):
        line = []
        for x in range(pieces):
            left = t * per_tap + x * (per_tap // pieces)
            for source in range(2 * parts):
                line.append(buf[source, :, left : left + size])
        updated = momentum_decay * momentum[t] + jnp.concatenate(line, axis=1)
        new_momentum[t] = updated
        new_weight[t] = weight[t] - learning_rate * updated


def update(place, weight, momentum, blocks, parts, pieces):
    weight, momentum = jnp.swapaxes(weight, 0, 1), jnp.swapaxes(momentum, 0, 1)
    taps, rows, chans = weight.shape
    lanes = blocks[0].shape[2]
    shape = jax.ShapeDtypeStruct(weight.shape, F32)
    own = pl.BlockSpec((taps // KERNEL, rows, chans), lambda a: (a, 0, 0))
    block = pl.BlockSpec((1, rows, lanes), lambda a: (a, 0, 0))
    results = pl.pallas_call(
        lambda *refs: update_kernel(parts, pieces, *refs),
        grid=(KERNEL,),
        out_shape=[shape, shape],
        in_specs=[SMEM, own, own] + [block] * len(blocks),
        out_specs=[own, own],
        scratch_shapes=[pltpu.VMEM((len(blocks), rows, lanes), F32)],
        compiler_params=SMALL,
    )(place, weight, momentum, *blocks)
    return tuple(jnp.swapaxes(result, 0, 1) for result in results)


def staged_gradient_kernel(count, mask, masks, slots, place, *refs):
    pieces = len(slots) - 2
    sources, refs = refs[: len(slots)], refs[len(slots) :]
    others, refs = refs[: len(masks)], refs[len(masks) :]
    gram_in, out, kept, gram_out, cot, win, sems = refs
    rows, size = sources[0].shape[1], sources[2].shape[1]
    rep, core, x = place[0], place[1], place[2]

    cot[2 * rows :, :] = jnp.zeros((cot.shape[0] - 2 * rows, cot.shape[1]), BF16)
    plane = HEIGHT * WIDTH
    for index in range(2):
        here = pl.ds(pl.multiple_of(jnp.bitwise_xor(core, index) * rows, 16), rows)
        for i in range(DEPTH):
            left = SPAN * i
            cot[here, left : left + plane] = sources[index][slots[index], :, plane * i : plane * (i + 1)]
            cot[here, left + plane : left + SPAN] = jnp.zeros((rows, SPAN - plane), BF16)
    for turn in range(pieces):

        @pl.when(x == turn)
        def _():
            for index in range(pieces):
                start = (turn ^ index) * size
                write_windows(sources[2 + index].at[slots[2 + index]], win, pieces * size, start)

    stores = []
    for a in range(KERNEL):
        product = lax.dot_general(
            cot[...],
            win[:, SPAN * a : SPAN * (a + DEPTH)],
            (((1,), (1,)), ((), ())),
            preferred_element_type=F32,
        )
        out[a] = product[: 2 * rows]
        stores.append(pltpu.make_async_copy(out.at[a], kept.at[a], sems.at[a]))
        stores[-1].start()

    lanes = out.shape[2]
    full, rest = lanes // LANES * LANES, lanes % LANES

    def body(step, sums):
        start = pl.multiple_of(step * 8, 8)
        sums = [list(pair) for pair in sums]
        for a in range(KERNEL):
            for left in range(0, full, LANES):
                mine = out[a, pl.ds(start, 8), left : left + LANES]
                for pair, ref in zip(sums, (*others, None)):
                    other = mine if ref is None else ref[a, pl.ds(start, 8), left : left + LANES]
                    pair[0] = pair[0] + mine * other
            if rest:
                mine = out[a, pl.ds(start, 8), full:]
                for pair, ref in zip(sums, (*others, None)):
                    other = mine if ref is None else ref[a, pl.ds(start, 8), full:]
                    pair[1] = pair[1] + mine * other
        return tuple(tuple(pair) for pair in sums)

    zero = (jnp.zeros((8, LANES), F32), jnp.zeros((8, max(rest, 1)), F32))
    sums = lax.fori_loop(0, 2 * rows // 8, body, (zero,) * (len(others) + 1))
    lane = lax.broadcasted_iota(jnp.int32, (1, LANES), 1)
    line = gram_in[...]
    first = jnp.bitwise_xor(rep, mask)
    for other, pair in zip((*masks, mask), sums):
        total = jnp.sum(pair[0]) + jnp.sum(pair[1])
        second = jnp.bitwise_xor(rep, other)
        here = (lane == first * count + second) | (lane == second * count + first)
        line = line + jnp.where(here, total, 0.0)
    gram_out[...] = jnp.broadcast_to(line, gram_out.shape)
    for store in stores:
        store.wait()


def staged_gradient(count, place, mask, cots, patches, before, gram, copies=None):
    _, rows, vox = cots[0][0].shape
    _, size, total = patches[0][0].shape
    chans = len(patches) * size
    taps = KERNEL * KERNEL
    operands = [*cots, *patches]
    shape = (KERNEL, 2 * rows, taps * chans)
    line = (1, LANES) if copies is None else (copies, 1, LANES)
    far = pl.BlockSpec(memory_space=pl.ANY)
    slots = [slot for _, slot in operands]
    return pl.pallas_call(
        lambda *refs: staged_gradient_kernel(count, mask, list(before), slots, *refs),
        out_shape=[pltpu.VMEM(shape, F32), pltpu.HBM(shape, F32), jax.ShapeDtypeStruct(line, F32)],
        in_specs=[SMEM] + [VMEM] * (len(operands) + len(before) + 1),
        out_specs=[VMEM, far, VMEM],
        scratch_shapes=[
            pltpu.VMEM((-(-2 * rows // 256) * 256, DEPTH * SPAN), BF16),
            pltpu.VMEM((taps * chans, PLANES * SPAN), BF16),
            pltpu.SemaphoreType.DMA((KERNEL,)),
        ],
        compiler_params=pltpu.CompilerParams(vmem_limit_bytes=14 * 2**20),
    )(place, *[in_vmem(array) for array, _ in operands], *[in_vmem(value) for value in before.values()], gram)


def staged_combine_kernel(count, place, gram, *refs):
    grads, outs = refs[:count], refs[count:-3]
    stage, factors, sems = refs[-3:]
    rows = outs[0].shape[1]
    half = len(outs) // 2
    copies = [
        [pltpu.make_async_copy(grad.at[a], stage.at[i, a], sems.at[i, a]) for i, grad in enumerate(grads)]
        for a in range(KERNEL)
    ]
    for group in copies:
        for copy in group:
            copy.start()
    total = gram[0]
    for device in range(1, gram.shape[0]):
        total = total + gram[device]
    products = lambda i, j: jnp.broadcast_to(total[:, i * count + j : i * count + j + 1], (1, LANES))
    for i, value in tree_weights(products, count).items():
        factors[i : i + 1, :] = value
    scales = [factors[pl.ds(jnp.bitwise_xor(place[0], i), 1), :][:, :1] for i in range(count)]
    for a in range(KERNEL):
        for copy in copies[a]:
            copy.wait()
        for index, out in enumerate(outs):
            core = jnp.bitwise_xor(index // half, place[1])
            low = jnp.bitwise_xor(index % half, place[3])
            here = pl.ds(pl.multiple_of((core * half + low) * rows, 8), rows)
            sums = scales[0] * stage[0, a, here, :]
            for i in range(1, count):
                sums = sums + scales[i] * stage[i, a, here, :]
            out[a] = sums


def staged_combine(place, gram, grads, blocks):
    step, rows, lanes = grads[0].shape
    shape = (step, rows // blocks, lanes)
    return pl.pallas_call(
        lambda *refs: staged_combine_kernel(len(grads), *refs),
        out_shape=[jax.ShapeDtypeStruct(shape, F32)] * blocks,
        in_specs=[SMEM, VMEM] + [pl.BlockSpec(memory_space=pl.ANY)] * len(grads),
        out_specs=[VMEM] * blocks,
        scratch_shapes=[
            pltpu.VMEM((len(grads),) + grads[0].shape, F32),
            pltpu.VMEM((len(grads), LANES), F32),
            pltpu.SemaphoreType.DMA((len(grads), step)),
        ],
        compiler_params=pltpu.CompilerParams(vmem_limit_bytes=30 * 2**20),
    )(place, gram, *[pltpu.with_memory_space_constraint(grad, pltpu.HBM) for grad in grads])


def staged_blocks(place, low, patch, kept, sent):
    count = lax.axis_size(REP)
    devices = count * lax.axis_size(CH)
    along = lambda value, mask: swap(value, REP, mask)
    across = lambda value: swap(value, "x", 1)
    core = lambda value: swap(value, "core", 1)
    join = lambda *values: jnp.concatenate(values)
    near, grads, gram = {}, {}, jnp.zeros((1, LANES), F32)

    def add(mask, cot, other, patch, far, cot_slot=0, other_slot=0, far_slot=0, copies=None):
        nonlocal gram
        operands = [(cot, cot_slot), (other, other_slot)], [(patch, 0), (far, far_slot)]
        near[mask], grads[mask], gram = staged_gradient(
            count, place, mask, *operands, near, gram, copies
        )

    cot0 = kept[None]
    cot4 = along(sent[None], 4)
    cot2 = along(cot0, 2)
    cot1 = along(cot0, 1)
    core0 = core(cot0)
    part0, part1, part2, part3 = pack_patch(low[None], patch, 4)
    part0, part1, core0 = hold_back([part0, part1, core0], [])
    far0 = across(part0)
    patch1 = along(part1, 1)

    part0, far0, patch1, cot1, cot2, cot4, part2 = hold_back(
        [part0, far0, patch1, cot1, cot2, cot4, part2], []
    )
    patch4 = along(part0, 4)
    far1 = across(patch1)
    core1 = core(cot1)
    cot35 = along(join(cot2, cot4), 1)
    patch2 = along(part2, 2)
    add(0, cot0, core0, part0, far0)

    part1, patch4, far1, core1, cot35, patch2, part3 = hold_back(
        [part1, patch4, far1, core1, cot35, patch2, part3], [gram]
    )
    patch5 = along(part1, 5)
    far24 = across(join(patch2, patch4))
    patch3 = along(part3, 3)
    core24 = core(join(cot2, cot4))
    add(1, cot1, core1, patch1, far1)

    part2, patch5, far24, patch3, core24 = hold_back([part2, patch5, far24, patch3, core24], [gram])
    patch6 = along(part2, 6)
    far35 = across(join(patch3, patch5))
    cot6 = along(cot4, 2)
    core35 = core(cot35)
    add(2, cot2, core24, patch2, far24)
    add(4, cot4, core24, patch4, far24, 0, 1, 1)

    part3, patch6, far35, cot6, core35 = hold_back([part3, patch6, far35, cot6, core35], [gram])
    patch7 = along(part3, 7)
    far6 = across(patch6)
    cot7 = along(cot6, 1)
    core6 = core(cot6)
    add(3, cot35, core35, patch3, far35)
    add(5, cot35, core35, patch5, far35, 1, 1, 1)

    patch7, far6, cot7, core6 = hold_back([patch7, far6, cot7, core6], [gram])
    far7 = across(patch7)
    core7 = core(cot7)
    add(6, cot6, core6, patch6, far6)
    far7, core7 = hold_back([far7, core7], [gram])
    add(7, cot7, core7, patch7, far7, copies=devices)

    gram = lax.all_to_all(gram, REP + CH, 0, 0, tiled=True)
    return staged_combine(place, gram, [grads[mask] for mask in range(count)], count)


def plain_gradients(place, low, patch, kept, sent):
    replicas, columns = lax.axis_size(REP), lax.axis_size(CH)
    parts, pieces = replicas // 2, columns // 2
    cots = {0: jnp.stack([kept, swap(sent, "half", 1)])}
    bit = parts // 2
    while bit:
        cots.update({mask | bit: swap(value, "low", bit) for mask, value in cots.items()})
        bit //= 2
    other_cots = {mask: swap(value, "core", 1) for mask, value in cots.items()}
    packed = pack_patch(low[None], patch, parts)
    grads = []
    for mask in range(replicas):
        part, slot = mask % parts, mask // parts
        mine = swap(packed[part], REP, mask) if mask else packed[part]
        spread = [mine] + [swap(mine, "x", other) for other in range(1, pieces)]
        grads.append(
            gradient_block(
                place, [(cots[part], slot), (other_cots[part], slot)], [(value, 0) for value in spread]
            )
        )
    return grads


def plain_blocks(place, low, patch, kept, sent):
    replicas, columns = lax.axis_size(REP), lax.axis_size(CH)
    grads = plain_gradients(place[1:3], low, patch, kept, sent)
    gram = gram_partial(place[:1], grads)
    devices = replicas * columns
    every = jnp.broadcast_to(gram, (devices,) + gram.shape)
    gram = lax.all_to_all(every, REP + CH, 0, 0, tiled=True).sum(0).reshape(-1)
    return combine_blocks(place, gram, grads, replicas)


def shards(patches, cotangents, weight, momentum):
    replicas, columns = lax.axis_size(REP), lax.axis_size(CH)
    parts, pieces = replicas // 2, columns // 2
    rep, upper, low = lax.axis_index(REP), lax.axis_index("half"), lax.axis_index("low")
    place = jnp.stack([rep, lax.axis_index("core"), lax.axis_index("x"), low])
    patch, cot = patches[0], cotangents[0]
    rows = cot.shape[0] // 2

    kept = lax.dynamic_slice_in_dim(cot, upper * rows, rows)
    sent = lax.dynamic_slice_in_dim(cot, (1 - upper) * rows, rows)
    result = staged_blocks if (replicas, columns) == (8, 4) else plain_blocks
    blocks = result(place, low, patch, kept, sent)
    blocks = [
        swap(block, ("low", "core"), index % parts * 2 + index // parts) if index else block
        for index, block in enumerate(blocks)
    ]
    return update(place, weight, momentum, blocks, parts, pieces)


def solution(mesh):
    replicas, columns = mesh.shape["rep"], mesh.shape["ch"]
    split = Mesh(mesh.devices.reshape(2, replicas // 2, columns // 2, 2), REP + CH)
    inputs, state = P(REP, CH, None), P(CH + REP, None, None)
    return jax.shard_map(
        shards, mesh=split, in_specs=(inputs, inputs, state, state), out_specs=(state, state), check_vma=False
    )
```

```python
import jax
import jax.numpy as jnp
from jax import lax
from jax.experimental import pallas as pl
from jax.experimental.pallas import tpu as pltpu
from jax.sharding import Mesh
from jax.sharding import PartitionSpec as P

KERNEL = 3
DEPTH = 6
HEIGHT = 14
WIDTH = 32
ROWS = HEIGHT + KERNEL - 1
CELLS = WIDTH + KERNEL - 1
PLANES = DEPTH + KERNEL - 1
SPAN = ROWS * WIDTH
LANES = 128
PER_VREG = LANES // WIDTH

momentum_decay = 0.9
learning_rate = 0.05

BF16 = jnp.bfloat16
F32 = jnp.float32
VMEM = pl.BlockSpec(memory_space=pltpu.VMEM)
SMEM = pl.BlockSpec(memory_space=pltpu.SMEM)
PARAMS = pltpu.CompilerParams(vmem_limit_bytes=56 * 2**20)
SMALL = pltpu.CompilerParams(vmem_limit_bytes=20 * 2**20)


REP = ("half", "low")
CH = ("x", "core")


def swap(value, axes, mask):
    pairs = [(source, source ^ mask) for source in range(lax.axis_size(axes))]
    return lax.ppermute(value, axes, pairs)


def in_vmem(value):
    return pltpu.with_memory_space_constraint(value, pltpu.VMEM)


def hold_back(values, until):
    values, until = list(values), list(until)
    here = pl.BlockSpec(memory_space=pl.ANY)
    return pl.pallas_call(
        lambda *refs: None,
        out_shape=[jax.ShapeDtypeStruct(value.shape, value.dtype) for value in values],
        in_specs=[here] * (len(values) + len(until)),
        out_specs=[here] * len(values),
        input_output_aliases={index: index for index in range(len(values))},
        compiler_params=pltpu.CompilerParams(vmem_limit_bytes=2**20),
    )(*values, *until)


def pack_kernel(low, patch_ref, *refs):
    parts, buf = refs[:-1], refs[-1]
    main = PLANES * SPAN
    for row in range(PLANES * ROWS):
        buf[:, WIDTH * row : WIDTH * (row + 1)] = patch_ref[:, CELLS * row : CELLS * row + WIDTH]
    total = PLANES * ROWS * CELLS
    tail = 2 * LANES
    k = lax.broadcasted_iota(jnp.int32, (total, tail), 0)
    n = lax.broadcasted_iota(jnp.int32, (total, tail), 1)
    lane = n % LANES
    row = PER_VREG * (lane % WIDTH) + lane // WIDTH
    pick = (k == row * CELLS + WIDTH + n // LANES).astype(BF16)
    buf[:, main:] = jnp.dot(patch_ref[...], pick, preferred_element_type=F32).astype(BF16)
    size = parts[0].shape[1]
    for mask, out in enumerate(parts):
        start = pl.multiple_of(jnp.bitwise_xor(low[0], mask) * size, 16)
        out[0] = buf[pl.ds(start, size), :]


def pack_patch(low, patch, parts):
    size = -(-patch.shape[0] // (16 * parts)) * 16
    if size * parts != patch.shape[0]:
        by_part = patch.reshape(parts, -1, patch.shape[1])
        by_part = jnp.pad(by_part, ((0, 0), (0, size - by_part.shape[1]), (0, 0)))
        patch = by_part.reshape(parts * size, -1)
    channels, total = patch.shape
    shape = jax.ShapeDtypeStruct((1, channels // parts, total), BF16)
    return pl.pallas_call(
        pack_kernel,
        out_shape=[shape] * parts,
        in_specs=[SMEM, VMEM],
        out_specs=[VMEM] * parts,
        scratch_shapes=[pltpu.VMEM((channels, total), BF16)],
        compiler_params=SMALL,
    )(low, patch)


def write_windows(pat, win, chans, start):
    size = pat.shape[0]
    main = PLANES * SPAN
    lane = lax.broadcasted_iota(jnp.int32, (size, LANES), 1) % WIDTH
    last, before = lane == WIDTH - 1, lane == WIDTH - 2
    first_tail, second_tail = pat[:, main : main + LANES], pat[:, main + LANES :]

    def window(b, e):
        return pl.ds((KERNEL * b + e) * chans + start, size)

    for q in range(main // LANES):
        here = slice(LANES * q, LANES * (q + 1))
        block = pat[:, here]
        to_last, to_before = (WIDTH - 1 - q) % LANES, (WIDTH - 2 - q) % LANES
        win[window(0, 0), here] = block
        win[window(0, 1), here] = jnp.where(
            last, pltpu.roll(first_tail, to_last, 1), pltpu.roll(block, LANES - 1, 1)
        )
        win[window(0, 2), here] = jnp.where(
            last,
            pltpu.roll(second_tail, to_last, 1),
            jnp.where(before, pltpu.roll(first_tail, to_before, 1), pltpu.roll(block, LANES - 2, 1)),
        )
    for e in range(KERNEL):
        for b in range(1, KERNEL):
            shift = WIDTH * b
            win[window(b, e), : main - shift] = win[window(0, e), shift:]
            win[window(b, e), main - shift :] = jnp.zeros((size, shift), BF16)


def gradient_kernel(pieces, place, *refs):
    cots, patches = refs[:2], refs[2 : 2 + pieces]
    out, cot, pat, win = refs[2 + pieces :]
    rows, size = cots[0].shape[0], patches[0].shape[0]
    chans = pieces * size
    core, x = place[0], place[1]
    plane = HEIGHT * WIDTH
    for index, ref in enumerate(cots):
        start = pl.multiple_of(jnp.bitwise_xor(core, index) * rows, 16)
        for i in range(DEPTH):
            cot[pl.ds(start, rows), SPAN * i : SPAN * i + plane] = ref[:, plane * i : plane * (i + 1)]
            cot[pl.ds(start, rows), SPAN * i + plane : SPAN * (i + 1)] = jnp.zeros((rows, SPAN - plane), BF16)
    for index, ref in enumerate(patches):
        start = pl.multiple_of(jnp.bitwise_xor(x, index) * size, 16)
        pat[pl.ds(start, size), :] = ref[...]

    write_windows(pat, win, chans, 0)
    for a in range(KERNEL):
        out[a] = lax.dot_general(
            cot[...],
            win[:, SPAN * a : SPAN * (a + DEPTH)],
            (((1,), (1,)), ((), ())),
            preferred_element_type=F32,
        )


def gradient_block(place, cots, patches):
    _, rows, vox = cots[0][0].shape
    _, size, total = patches[0][0].shape
    chans = len(patches) * size
    taps = KERNEL * KERNEL

    def part(array, slot):
        return pl.BlockSpec((None,) + array.shape[1:], lambda i: (slot, 0, 0))

    operands = [*cots, *patches]
    return pl.pallas_call(
        lambda *refs: gradient_kernel(len(patches), *refs),
        grid=(1,),
        out_shape=jax.ShapeDtypeStruct((KERNEL, 2 * rows, taps * chans), F32),
        in_specs=[SMEM] + [part(*operand) for operand in operands],
        out_specs=pl.BlockSpec((KERNEL, 2 * rows, taps * chans), lambda i: (0, 0, 0)),
        scratch_shapes=[
            pltpu.VMEM((2 * rows, DEPTH * SPAN), BF16),
            pltpu.VMEM((chans, total), BF16),
            pltpu.VMEM((taps * chans, PLANES * SPAN), BF16),
        ],
        compiler_params=PARAMS,
    )(place, *[array for array, _ in operands])


def gram_kernel(rep, *refs):
    grads, out = refs[:-1], refs[-1]
    count = len(grads)
    step, rows, lanes = grads[0].shape
    group = min(count, 8)

    @pl.when(pl.program_id(0) == 0)
    def _():
        out[...] = jnp.zeros_like(out)

    lane = lax.broadcasted_iota(jnp.int32, (1, LANES), 1)
    for first in range(0, count, group):
        for second in range(0, first + 1, group):
            pairs = [
                (i, j)
                for i in range(first, first + group)
                for j in range(second, min(second + group, i + 1))
            ]

            def body(r, sums):
                start = pl.multiple_of(r * 8, 8)
                sums = list(sums)
                for left in range(0, lanes, LANES):
                    width = min(LANES, lanes - left)
                    need = sorted({i for pair in pairs for i in pair})
                    tile = {i: grads[i][0, pl.ds(start, 8), left : left + width] for i in need}
                    for n, (i, j) in enumerate(pairs):
                        product = tile[i] * tile[j]
                        if width < LANES:
                            product = jnp.pad(product, ((0, 0), (0, LANES - width)))
                        sums[n] = sums[n] + product
                return tuple(sums)

            zero = jnp.zeros((8, LANES), F32)
            sums = lax.fori_loop(0, rows // 8, body, (zero,) * len(pairs))
            for (i, j), value in zip(pairs, sums):
                total = jnp.sum(value)
                a, b = jnp.bitwise_xor(rep[0], i), jnp.bitwise_xor(rep[0], j)
                for at in [a * count + b, b * count + a][: 1 + (i != j)]:
                    out[pl.ds(at // LANES, 1), :] += jnp.where(lane == at % LANES, total, 0.0)


def gram_partial(rep, grads):
    count = len(grads)
    step, rows, lanes = grads[0].shape
    out_rows = -(-count * count // LANES)
    return pl.pallas_call(
        gram_kernel,
        grid=(step,),
        out_shape=jax.ShapeDtypeStruct((out_rows, LANES), F32),
        in_specs=[SMEM] + [pl.BlockSpec((1, rows, lanes), lambda i: (i, 0, 0))] * count,
        out_specs=pl.BlockSpec((out_rows, LANES), lambda i: (0, 0)),
        compiler_params=PARAMS,
    )(rep, *grads)


def tree_weights(gram, count):
    def inner(left, right):
        total = 0.0
        for i, u in left.items():
            part = 0.0
            for j, v in right.items():
                part = part + v * gram(i, j)
            total = total + u * part
        return total

    def combine(low, level):
        if 2**level == count:
            return {low: jnp.ones((1, LANES), F32)}
        former, latter = combine(low, level + 1), combine(low + 2**level, level + 1)
        dot = inner(former, latter)
        scale_former = 1.0 - dot / (2.0 * inner(former, former))
        scale_latter = 1.0 - dot / (2.0 * inner(latter, latter))
        joined = {i: scale_former * u for i, u in former.items()}
        joined.update({i: scale_latter * v for i, v in latter.items()})
        return joined

    return combine(0, 0)


def combine_kernel(count, place, gram, *refs):
    grads, outs, factors = refs[:count], refs[count:-1], refs[-1]
    step = pl.program_id(0)

    @pl.when(step == 0)
    def _():
        weights = tree_weights(lambda i, j: jnp.full((1, LANES), gram[i * count + j]), count)
        for i, value in weights.items():
            factors[i : i + 1, :] = value

    scales = [factors[pl.ds(jnp.bitwise_xor(place[0], i), 1), :][:, :1] for i in range(count)]
    for index, out in enumerate(outs):

        @pl.when(step == index)
        def _():
            for a in range(KERNEL):
                total = scales[0] * grads[0][a, 0]
                for scale, grad in zip(scales[1:], grads[1:]):
                    total = total + scale * grad[a, 0]
                out[a] = total


def combine_blocks(place, gram, grads, blocks):
    count = len(grads)
    step, rows, lanes = grads[0].shape
    grads = [grad.reshape(step, blocks, rows // blocks, lanes) for grad in grads]
    half = blocks // 2

    def index(i, place):
        core = jnp.bitwise_xor(i // half, place[1])
        low = jnp.bitwise_xor(i % half, place[3])
        return (0, core * half + low, 0, 0)

    block = pl.BlockSpec((step, 1, rows // blocks, lanes), index)
    out_shape = (step, rows // blocks, lanes)
    return pl.pallas_call(
        lambda *refs: combine_kernel(count, *refs),
        grid_spec=pltpu.PrefetchScalarGridSpec(
            num_scalar_prefetch=1,
            grid=(blocks,),
            in_specs=[SMEM] + [block] * count,
            out_specs=[pl.BlockSpec(out_shape, lambda i, place: (0, 0, 0))] * blocks,
            scratch_shapes=[pltpu.VMEM((count, LANES), F32)],
        ),
        out_shape=[jax.ShapeDtypeStruct(out_shape, F32)] * blocks,
        compiler_params=PARAMS,
    )(place, gram, *grads)


def update_kernel(parts, pieces, place, weight, momentum, *refs):
    blocks, (new_weight, new_momentum, buf) = refs[:-3], refs[-3:]
    taps = KERNEL * KERNEL
    per_tap = blocks[0].shape[2] // taps
    size = weight.shape[2] // (2 * parts * pieces)
    for index, ref in enumerate(blocks):
        core = jnp.bitwise_xor(index // parts, place[1])
        low = jnp.bitwise_xor(index % parts, place[3])
        buf[core * parts + low] = ref[0]
    for turn in range(pieces):

        @pl.when(place[2] == turn)
        def _():
            for t in range(taps):
                line = []
                for x in range(pieces):
                    left = t * per_tap + (x ^ turn) * (per_tap // pieces)
                    for source in range(2 * parts):
                        line.append(buf[source, :, left : left + size])
                updated = momentum_decay * momentum[t] + jnp.concatenate(line, axis=1)
                new_momentum[t] = updated
                new_weight[t] = weight[t] - learning_rate * updated


def update(place, weight, momentum, blocks, parts, pieces):
    weight, momentum = jnp.swapaxes(weight, 0, 1), jnp.swapaxes(momentum, 0, 1)
    taps, rows, chans = weight.shape
    lanes = blocks[0].shape[2]
    shape = jax.ShapeDtypeStruct(weight.shape, F32)
    own = pl.BlockSpec((taps // KERNEL, rows, chans), lambda a: (a, 0, 0))
    block = pl.BlockSpec((1, rows, lanes), lambda a: (a, 0, 0))
    results = pl.pallas_call(
        lambda *refs: update_kernel(parts, pieces, *refs),
        grid=(KERNEL,),
        out_shape=[shape, shape],
        in_specs=[SMEM, own, own] + [block] * len(blocks),
        out_specs=[own, own],
        scratch_shapes=[pltpu.VMEM((len(blocks), rows, lanes), F32)],
        compiler_params=SMALL,
    )(place, weight, momentum, *blocks)
    return tuple(jnp.swapaxes(result, 0, 1) for result in results)


def staged_gradient_kernel(count, mask, masks, slots, place, *refs):
    pieces = len(slots) - 2
    sources, refs = refs[: len(slots)], refs[len(slots) :]
    others, refs = refs[: len(masks)], refs[len(masks) :]
    gram_in, out, kept, gram_out, cot, win, sems = refs
    rows, size = sources[0].shape[1], sources[2].shape[1]
    rep = place[0]

    cot[2 * rows :, :] = jnp.zeros((cot.shape[0] - 2 * rows, cot.shape[1]), BF16)
    plane = HEIGHT * WIDTH
    for index in range(2):
        here = slice(index * rows, (index + 1) * rows)
        for i in range(DEPTH):
            left = SPAN * i
            cot[here, left : left + plane] = sources[index][slots[index], :, plane * i : plane * (i + 1)]
            cot[here, left + plane : left + SPAN] = jnp.zeros((rows, SPAN - plane), BF16)
    for index in range(pieces):
        write_windows(sources[2 + index].at[slots[2 + index]], win, pieces * size, index * size)
    stores = []
    for a in range(KERNEL):
        product = lax.dot_general(
            cot[...],
            win[:, SPAN * a : SPAN * (a + DEPTH)],
            (((1,), (1,)), ((), ())),
            preferred_element_type=F32,
        )
        out[a] = product[: 2 * rows]
        stores.append(pltpu.make_async_copy(out.at[a], kept.at[a], sems.at[a]))
        stores[-1].start()

    lanes = out.shape[2]
    full, rest = lanes // LANES * LANES, lanes % LANES

    def body(step, sums):
        start = pl.multiple_of(step * 8, 8)
        sums = [list(pair) for pair in sums]
        for a in range(KERNEL):
            for left in range(0, full, LANES):
                mine = out[a, pl.ds(start, 8), left : left + LANES]
                for pair, ref in zip(sums, (*others, None)):
                    other = mine if ref is None else ref[a, pl.ds(start, 8), left : left + LANES]
                    pair[0] = pair[0] + mine * other
            if rest:
                mine = out[a, pl.ds(start, 8), full:]
                for pair, ref in zip(sums, (*others, None)):
                    other = mine if ref is None else ref[a, pl.ds(start, 8), full:]
                    pair[1] = pair[1] + mine * other
        return tuple(tuple(pair) for pair in sums)

    zero = (jnp.zeros((8, LANES), F32), jnp.zeros((8, max(rest, 1)), F32))
    sums = lax.fori_loop(0, 2 * rows // 8, body, (zero,) * (len(others) + 1))
    lane = lax.broadcasted_iota(jnp.int32, (1, LANES), 1)
    line = gram_in[...]
    first = jnp.bitwise_xor(rep, mask)
    for other, pair in zip((*masks, mask), sums):
        total = jnp.sum(pair[0]) + jnp.sum(pair[1])
        second = jnp.bitwise_xor(rep, other)
        here = (lane == first * count + second) | (lane == second * count + first)
        line = line + jnp.where(here, total, 0.0)
    gram_out[...] = jnp.broadcast_to(line, gram_out.shape)
    for store in stores:
        store.wait()


def staged_gradient(count, place, mask, cots, patches, before, gram, copies=None):
    _, rows, vox = cots[0][0].shape
    _, size, total = patches[0][0].shape
    chans = len(patches) * size
    taps = KERNEL * KERNEL
    operands = [*cots, *patches]
    shape = (KERNEL, 2 * rows, taps * chans)
    line = (1, LANES) if copies is None else (copies, 1, LANES)
    far = pl.BlockSpec(memory_space=pl.ANY)
    slots = [slot for _, slot in operands]
    return pl.pallas_call(
        lambda *refs: staged_gradient_kernel(count, mask, list(before), slots, *refs),
        out_shape=[pltpu.VMEM(shape, F32), pltpu.HBM(shape, F32), jax.ShapeDtypeStruct(line, F32)],
        in_specs=[SMEM] + [VMEM] * (len(operands) + len(before) + 1),
        out_specs=[VMEM, far, VMEM],
        scratch_shapes=[
            pltpu.VMEM((-(-2 * rows // 256) * 256, DEPTH * SPAN), BF16),
            pltpu.VMEM((taps * chans, PLANES * SPAN), BF16),
            pltpu.SemaphoreType.DMA((KERNEL,)),
        ],
        compiler_params=pltpu.CompilerParams(vmem_limit_bytes=14 * 2**20),
    )(place, *[in_vmem(array) for array, _ in operands], *[in_vmem(value) for value in before.values()], gram)


def staged_combine_kernel(count, place, gram, *refs):
    grads, outs = refs[:count], refs[count:-3]
    stage, factors, sems = refs[-3:]
    rows = outs[0].shape[1]
    half = len(outs) // 2
    copies = [
        [pltpu.make_async_copy(grad.at[a], stage.at[i, a], sems.at[i, a]) for i, grad in enumerate(grads)]
        for a in range(KERNEL)
    ]
    for group in copies:
        for copy in group:
            copy.start()
    total = gram[0]
    for device in range(1, gram.shape[0]):
        total = total + gram[device]
    products = lambda i, j: jnp.broadcast_to(total[:, i * count + j : i * count + j + 1], (1, LANES))
    for i, value in tree_weights(products, count).items():
        factors[i : i + 1, :] = value
    scales = [factors[pl.ds(jnp.bitwise_xor(place[0], i), 1), :][:, :1] for i in range(count)]
    for a in range(KERNEL):
        for copy in copies[a]:
            copy.wait()
        for index, out in enumerate(outs):
            low = jnp.bitwise_xor(index % half, place[3])
            here = pl.ds(pl.multiple_of((index // half * half + low) * rows, 8), rows)
            sums = scales[0] * stage[0, a, here, :]
            for i in range(1, count):
                sums = sums + scales[i] * stage[i, a, here, :]
            out[a] = sums


def staged_combine(place, gram, grads, blocks):
    step, rows, lanes = grads[0].shape
    shape = (step, rows // blocks, lanes)
    return pl.pallas_call(
        lambda *refs: staged_combine_kernel(len(grads), *refs),
        out_shape=[jax.ShapeDtypeStruct(shape, F32)] * blocks,
        in_specs=[SMEM, VMEM] + [pl.BlockSpec(memory_space=pl.ANY)] * len(grads),
        out_specs=[VMEM] * blocks,
        scratch_shapes=[
            pltpu.VMEM((len(grads),) + grads[0].shape, F32),
            pltpu.VMEM((len(grads), LANES), F32),
            pltpu.SemaphoreType.DMA((len(grads), step)),
        ],
        compiler_params=pltpu.CompilerParams(vmem_limit_bytes=30 * 2**20),
    )(place, gram, *[pltpu.with_memory_space_constraint(grad, pltpu.HBM) for grad in grads])


def staged_blocks(place, low, patch, kept, sent):
    count = lax.axis_size(REP)
    devices = count * lax.axis_size(CH)
    along = lambda value, mask: swap(value, REP, mask)
    across = lambda value: swap(value, "x", 1)
    core = lambda value: swap(value, "core", 1)
    join = lambda *values: jnp.concatenate(values)
    near, grads, gram = {}, {}, jnp.zeros((1, LANES), F32)

    def add(mask, cot, other, patch, far, cot_slot=0, other_slot=0, far_slot=0, copies=None):
        nonlocal gram
        operands = [(cot, cot_slot), (other, other_slot)], [(patch, 0), (far, far_slot)]
        near[mask], grads[mask], gram = staged_gradient(
            count, place, mask, *operands, near, gram, copies
        )

    cot0 = kept[None]
    cot4 = along(sent[None], 4)
    cot2 = along(cot0, 2)
    cot1 = along(cot0, 1)
    core0 = core(cot0)
    part0, part1, part2, part3 = pack_patch(low[None], patch, 4)
    part0, part1, core0 = hold_back([part0, part1, core0], [])
    far0 = across(part0)
    patch1 = along(part1, 1)

    part0, far0, patch1, cot1, cot2, cot4, part2 = hold_back(
        [part0, far0, patch1, cot1, cot2, cot4, part2], []
    )
    patch4 = along(part0, 4)
    far1 = across(patch1)
    core1 = core(cot1)
    cot35 = along(join(cot2, cot4), 1)
    patch2 = along(part2, 2)
    add(0, cot0, core0, part0, far0)

    part1, patch4, far1, core1, cot35, patch2, part3 = hold_back(
        [part1, patch4, far1, core1, cot35, patch2, part3], [gram]
    )
    patch5 = along(part1, 5)
    far24 = across(join(patch2, patch4))
    patch3 = along(part3, 3)
    core24 = core(join(cot2, cot4))
    add(1, cot1, core1, patch1, far1)

    part2, patch5, far24, patch3, core24 = hold_back([part2, patch5, far24, patch3, core24], [gram])
    patch6 = along(part2, 6)
    far35 = across(join(patch3, patch5))
    cot6 = along(cot4, 2)
    core35 = core(cot35)
    add(2, cot2, core24, patch2, far24)
    add(4, cot4, core24, patch4, far24, 0, 1, 1)

    part3, patch6, far35, cot6, core35 = hold_back([part3, patch6, far35, cot6, core35], [gram])
    patch7 = along(part3, 7)
    far6 = across(patch6)
    cot7 = along(cot6, 1)
    core6 = core(cot6)
    add(3, cot35, core35, patch3, far35)
    add(5, cot35, core35, patch5, far35, 1, 1, 1)

    patch7, far6, cot7, core6 = hold_back([patch7, far6, cot7, core6], [gram])
    far7 = across(patch7)
    core7 = core(cot7)
    add(6, cot6, core6, patch6, far6)
    far7, core7 = hold_back([far7, core7], [gram])
    add(7, cot7, core7, patch7, far7, copies=devices)

    gram = lax.all_to_all(gram, REP + CH, 0, 0, tiled=True)
    return staged_combine(place, gram, [grads[mask] for mask in range(count)], count)


def plain_gradients(place, low, patch, kept, sent):
    replicas, columns = lax.axis_size(REP), lax.axis_size(CH)
    parts, pieces = replicas // 2, columns // 2
    cots = {0: jnp.stack([kept, swap(sent, "half", 1)])}
    bit = parts // 2
    while bit:
        cots.update({mask | bit: swap(value, "low", bit) for mask, value in cots.items()})
        bit //= 2
    other_cots = {mask: swap(value, "core", 1) for mask, value in cots.items()}
    packed = pack_patch(low[None], patch, parts)
    grads = []
    for mask in range(replicas):
        part, slot = mask % parts, mask // parts
        mine = swap(packed[part], REP, mask) if mask else packed[part]
        spread = [mine] + [swap(mine, "x", other) for other in range(1, pieces)]
        grads.append(
            gradient_block(
                place, [(cots[part], slot), (other_cots[part], slot)], [(value, 0) for value in spread]
            )
        )
    return grads


def plain_blocks(place, low, patch, kept, sent):
    replicas, columns = lax.axis_size(REP), lax.axis_size(CH)
    grads = plain_gradients(place[1:3], low, patch, kept, sent)
    gram = gram_partial(place[:1], grads)
    devices = replicas * columns
    every = jnp.broadcast_to(gram, (devices,) + gram.shape)
    gram = lax.all_to_all(every, REP + CH, 0, 0, tiled=True).sum(0).reshape(-1)
    return combine_blocks(place, gram, grads, replicas)


def shards(patches, cotangents, weight, momentum):
    replicas, columns = lax.axis_size(REP), lax.axis_size(CH)
    parts, pieces = replicas // 2, columns // 2
    rep, upper, low = lax.axis_index(REP), lax.axis_index("half"), lax.axis_index("low")
    place = jnp.stack([rep, lax.axis_index("core"), lax.axis_index("x"), low])
    patch, cot = patches[0], cotangents[0]
    rows = cot.shape[0] // 2

    kept = lax.dynamic_slice_in_dim(cot, upper * rows, rows)
    sent = lax.dynamic_slice_in_dim(cot, (1 - upper) * rows, rows)
    if (replicas, columns) == (8, 4):
        blocks = staged_blocks(place, low, patch, kept, sent)
    else:
        blocks = plain_blocks(place, low, patch, kept, sent)
        place = place.at[2].set(0)
    blocks = [
        swap(block, ("low", "core"), index % parts * 2 + index // parts) if index else block
        for index, block in enumerate(blocks)
    ]
    return update(place, weight, momentum, blocks, parts, pieces)


def solution(mesh):
    replicas, columns = mesh.shape["rep"], mesh.shape["ch"]
    split = Mesh(mesh.devices.reshape(2, replicas // 2, columns // 2, 2), REP + CH)
    inputs, state = P(REP, CH, None), P(CH + REP, None, None)
    return jax.shard_map(
        shards, mesh=split, in_specs=(inputs, inputs, state, state), out_specs=(state, state), check_vma=False
    )
```
